128 devices in a mesh: band: 4 (over z_hi, core), dom: 32 (over y, z_lo, x).
Axes of the slice: x: 4, y: 4, z: 4 (z_hi: 2, z_lo: 2; z = z_hi * 2 + z_lo), core: 2. Of those that a mesh axis runs over, the one named last changes fastest.
Arguments:
- orbitals: bfloat16 [512, 128, 32, 256], P('band', 'dom'), may hold values from -0.1875 to 0.1875
- potential: float32 [128, 32, 256], P('dom'), may hold values from 0.5 to 2.5
- projectors: bfloat16 [128, 128, 32, 256], P(None, 'dom'), may hold values from -0.1875 to 0.1875
- coupling: float32 [128], replicated, may hold values from -1 to 1
- pattern: int32 [8, 2], P('band'), may hold values 0 or 1
Outputs:
- correlation_next: float32 [512, 128], P(('band', 'dom'))
- hamiltonian_next: float32 [512, 128], P(('band', 'dom'))
The draws below stay inside these ranges and needn't reach their ends.
All inputs are finite; a program needn't handle non-finite values. No bound on the sum of `pattern` on one device may be relied on, other than what follows from the above.
Results may differ from the reference program's by a relative error of at most 0.0033.
The reference program's roundings to bfloat16 on the way (of `weighted` and `images`) count: a program that leaves them out, or rounds other values in their place, can miss the bound.
Values may be sent and summed in bfloat16 or wider, within the bound.
A program may use at most 384 MiB of HBM per device.

```python
import jax
import jax.numpy as jnp
from jax import lax

BLOCK = 64
ORB_DEV = 128
NY = 32
NZ = 256
NPROJ = 128
NX = 128
ORB = 512
NBLK = 8
BPG = 2
N_BAND = 4


def set_ends(drawn, own_key, low, high):
    index_at = [jax.random.randint(jax.random.fold_in(own_key, axis), (), 0, length) for axis, length in enumerate(drawn.shape)]
    main_axis = drawn.shape.index(max(drawn.shape))
    next_to = index_at[:main_axis] + [(index_at[main_axis] + 1) % drawn.shape[main_axis]] + index_at[main_axis + 1:]
    return drawn.at[tuple(index_at)].set(low).at[tuple(next_to)].set(high)


def level_of(rng, extent, cuts, smallest, high):
    gain = 1.0
    for dim, blocks in cuts:
        heights = jax.random.uniform(jax.random.fold_in(jax.random.fold_in(rng, 6), dim), (blocks,), jnp.float32, smallest / len(cuts), high / len(cuts))
        gain = gain * jnp.repeat(jnp.exp(heights), extent[dim] // blocks).reshape((-1,) + (1,) * (len(extent) - 1 - dim))
    return gain


def gaussian(own_key, extent, scale, limit, pieces=(), dtype=jnp.bfloat16):
    level = level_of(own_key, extent, pieces, -0.22, 0.18) if pieces else 1.0
    result = jax.random.normal(own_key, extent, jnp.float32) * scale * level
    return jnp.minimum(jnp.maximum(result, -limit), limit).astype(dtype)


def setup_inputs(seed: int = 0) -> dict:
    splits = jax.random.split(jax.random.key(seed), 6)
    orbitals = gaussian(splits[0], (ORB, NX, NY, NZ), (1.0 / (NX * NY * NZ) ** 0.25), 0.1875, ((0, 4), (1, 32)))
    potential = jnp.clip(0.5 + 2.0 * jax.random.uniform(splits[1], (NX, NY, NZ), jnp.float32) ** level_of(splits[1], (NX, NY, NZ), ((0, 32),), -0.2, 0.2), 0.5, 2.5)
    projectors = gaussian(splits[2], (NPROJ, NX, NY, NZ), (1.0 / (NX * NY * NZ) ** 0.25), 0.1875, ((1, 32),))
    coupling = jnp.clip(jax.random.uniform(splits[3], (NPROJ,), jnp.float32, -1.0, 1.0), -1.0, 1.0)
    pattern = set_ends((jax.random.randint(splits[4], (NBLK, BPG), 0, 3) < 2).astype(jnp.int32), jax.random.fold_in(splits[4], 1), 0, 1)
    return dict(orbitals=orbitals, potential=potential, projectors=projectors, coupling=coupling, pattern=pattern)


C0 = -2.5
C1 = 4.0 / 3.0
C2 = -1.0 / 12.0


def apply_block(block, potential, proj_flat, coupling):
    field = block.astype(jnp.float32)
    near = jnp.zeros_like(field)
    far = jnp.zeros_like(field)
    for axis in (1, 2, 3):
        near = near + jnp.roll(field, 1, axis) + jnp.roll(field, -1, axis)
        far = far + jnp.roll(field, 2, axis) + jnp.roll(field, -2, axis)
    kinetic = -0.5 * (3.0 * C0 * field + C1 * near + C2 * far)
    local = potential[None] * field
    flat = block.reshape(block.shape[0], -1)
    coef = jnp.dot(proj_flat, flat.T, preferred_element_type=jnp.float32)
    weighted = (coupling[:, None] * coef).astype(jnp.bfloat16)
    nonlocal_part = jnp.dot(weighted.T, proj_flat, preferred_element_type=jnp.float32)
    total = kinetic.reshape(block.shape[0], -1) + local.reshape(block.shape[0], -1) + nonlocal_part
    return total.astype(jnp.bfloat16)


def reference(orbitals, potential, projectors, coupling, pattern):
    proj_flat = projectors.reshape(NPROJ, -1)
    blocks = orbitals.reshape(NBLK, BLOCK, NX, NY, NZ)
    images = lax.map(lambda blk: apply_block(blk, potential, proj_flat, coupling), blocks)
    images = images.reshape(ORB, -1)
    flat = orbitals.reshape(ORB, -1)
    mask = jnp.repeat(jnp.repeat(pattern.astype(jnp.float32), BLOCK, 0), BLOCK, 1)
    correlations = []
    hams = []
    for group in range(N_BAND):
        after = (group + 1) % N_BAND
        left = flat[group * ORB_DEV:(group + 1) * ORB_DEV]
        right = flat[after * ORB_DEV:(after + 1) * ORB_DEV]
        right_img = images[after * ORB_DEV:(after + 1) * ORB_DEV]
        correlations.append(jnp.dot(left, right.T, preferred_element_type=jnp.float32))
        hams.append(jnp.dot(left, right_img.T, preferred_element_type=jnp.float32))
    correlation_next = jnp.concatenate(correlations, 0) * mask
    hamiltonian_next = jnp.concatenate(hams, 0) * mask
    return correlation_next, hamiltonian_next
```

```python
import functools

import jax
import jax.numpy as jnp
from jax import lax
from jax.experimental import pallas as pl
from jax.experimental.pallas import tpu as pltpu
from jax.sharding import PartitionSpec as P

W_CENTER = 90.0
W_NEAR = -16.0
W_FAR = 1.0
W_SCALE = 1.0 / 24.0

MESH = pl.DeviceIdType.MESH
CHUNK = 16
PLANES = 4
PARTS = 8


def dot_rows(left, right):
    return lax.dot_general(left, right, (((1,), (1,)), ((), ())), preferred_element_type=jnp.float32)


def kernel(
    orb_hbm, proj_hbm, pot, coupling, pattern, corr_out, ham_out,
    nat, pnat, pt, ext, img, other, circ, coef, acc,
    rc, s1c, qc, s2c, tc, nb, rr, s1, qq, s2,
    in_sem, pin_sem, halo_s, halo_r, pair_s, pair_r, cross_s, cross_r,
    c1_s, c1_r, c2_s, c2_r, n_s, n_r, f1_s, f1_r, f2_s, f2_r,
):
    band = lax.axis_index("band")
    dom = lax.axis_index("dom")
    core = lax.rem(band, 2)
    zh = band // 2
    yz = dom // 4
    xx = lax.rem(dom, 4)
    partner = zh * 2 + (1 - core)
    cross = (1 - zh) * 2 + (1 - core)
    is_even = core == 0
    is_odd = core == 1

    def x_peer(j):
        return yz * 4 + lax.rem(xx + j, 4)

    def yz_peer(j):
        return lax.rem(yz + j, 8) * 4 + xx

    def remote(src, dst, ssem, rsem, to_band, to_dom):
        return pltpu.make_async_remote_copy(
            src_ref=src, dst_ref=dst, send_sem=ssem, recv_sem=rsem,
            device_id=(to_band, to_dom), device_id_type=MESH,
        )

    def plane_of(k):
        return lax.rem(k, 2) * 2 + k // 4

    def rows_of(k):
        return pl.ds(pl.multiple_of(lax.rem(k // 2, 2) * CHUNK, CHUNK), CHUNK)

    def load(src, dst, sem, k):
        return pltpu.make_async_copy(src.at[:, plane_of(k), rows_of(k), :], dst.at[lax.rem(k, 2)], sem.at[lax.rem(k, 2)])

    def own(k):
        return ext.at[plane_of(k) + 2, rows_of(k)]

    def halo(k):
        side = lax.rem(k, 2)
        to_dom = lax.rem(dom + 31 + 2 * side, 32)
        return remote(own(k), ext.at[plane_of(k) + 6 - 8 * side, rows_of(k)], halo_s.at[k], halo_r.at[k], band, to_dom)

    def to_pair(k):
        return remote(own(k), other.at[plane_of(k), rows_of(k), pl.ds(0, 128)], pair_s.at[k], pair_r.at[k], partner, dom)

    def to_cross(k):
        return remote(own(k), other.at[plane_of(k), rows_of(k), pl.ds(128, 128)], cross_s.at[k], cross_r.at[k], cross, dom)

    load(orb_hbm, nat, in_sem, 0).start()
    load(proj_hbm, pnat, pin_sem, 0).start()

    barrier = pltpu.get_barrier_semaphore()
    peers = [(band, x_peer(j)) for j in (1, 2, 3)]
    peers += [(band, yz_peer(j)) for j in range(1, 8)]
    peers += [(cross, yz_peer(j)) for j in range(8)]
    peers += [(partner, dom), (band, lax.rem(dom + 1, 32)), (band, lax.rem(dom + 31, 32))]
    for peer in peers:
        pl.semaphore_signal(barrier, inc=1, device_id=peer, device_id_type=MESH)

    row = lax.broadcasted_iota(jnp.int32, (256, 256), 0)
    col = lax.broadcasted_iota(jnp.int32, (256, 256), 1)
    gap = (row - col) & 255
    near_z = (gap == 1) | (gap == 255)
    far_z = (gap == 2) | (gap == 254)
    circ[...] = jnp.where(gap == 0, W_CENTER, jnp.where(near_z, W_NEAR, jnp.where(far_z, W_FAR, 0.0))).astype(jnp.bfloat16)
    coef[...] = jnp.zeros_like(coef)
    rc[...] = jnp.zeros_like(rc)

    pl.semaphore_wait(barrier, len(peers))

    @pl.loop(0, PARTS)
    def _(k):
        slot = lax.rem(k, 2)

        @pl.when(k + 1 < PARTS)
        def _():
            load(orb_hbm, nat, in_sem, k + 1).start()
            load(proj_hbm, pnat, pin_sem, k + 1).start()

        load(orb_hbm, nat, in_sem, k).wait()
        px = plane_of(k) + 2
        rows = rows_of(k)

        @pl.loop(0, 8)
        def _(q):
            r = pl.ds(pl.multiple_of(q * 16, 16), 16)
            ext[px, rows, r, :] = jnp.swapaxes(nat[slot, r], 0, 1)

        @pl.when(is_even)
        def _():
            halo(k).start()

        @pl.when(is_odd)
        def _():
            to_cross(k).start()
            to_pair(k).start()

        load(proj_hbm, pnat, pin_sem, k).wait()

        @pl.loop(0, 8)
        def _(q):
            r = pl.ds(pl.multiple_of(q * 16, 16), 16)
            pt[:, r, :] = jnp.swapaxes(pnat[slot, r], 0, 1)

        first = lax.rem(k // 2, 2) * CHUNK
        part = coef[...]
        for r in range(CHUNK):
            part = part + dot_rows(pt[r], ext[px, first + r])
        coef[...] = part

    for d in range(32):
        rc[d % 4, d // 4, 0:4, :] = coef[4 * d:4 * d + 4, :]

    def c1(j):
        return remote(rc.at[lax.rem(xx + j, 4)], s1c.at[j], c1_s.at[j], c1_r.at[j], band, x_peer(j))

    def c2(j):
        return remote(qc.at[lax.rem(yz + j, 8)], s2c.at[j], c2_s.at[j], c2_r.at[j], band, yz_peer(j))

    def n_pair():
        return remote(tc, nb.at[0], n_s.at[0], n_r.at[0], partner, dom)

    def n_cross():
        return remote(tc, nb.at[1], n_s.at[1], n_r.at[1], cross, dom)

    for j in (1, 2, 3):
        c1(j).start()

    def local_rows(start, stop):
        def body(k, carry):
            x = k // 32
            y = lax.rem(k, 32)

            def at(dx, dy):
                return ext[x + 2 + dx, lax.rem(y + 32 + dy, 32)].astype(jnp.float32)

            center = ext[x + 2, y]
            own_z = jnp.dot(center, circ[...], preferred_element_type=jnp.float32)
            near = (at(-1, 0) + at(1, 0)) + (at(0, -1) + at(0, 1))
            far = (at(-2, 0) + at(2, 0)) + (at(0, -2) + at(0, 2))
            kinetic = (own_z + W_NEAR * near + far) * W_SCALE
            img[x, y] = (kinetic + pot[x, pl.ds(y, 1), :] * center.astype(jnp.float32)).astype(jnp.bfloat16)
            return carry

        lax.fori_loop(start, stop, body, 0)

    @pl.when(is_even)
    def _():
        for k in (1, 3, 5, 7):
            halo(k).wait_recv()
        local_rows(0, 64)

    def sum_c1():
        for j in (1, 2, 3):
            c1(j).wait_recv()
        qc[...] = (rc[xx] + s1c[1]) + (s1c[2] + s1c[3])
        for j in range(1, 8):
            c2(j).start()

    def sum_c2():
        for j in range(1, 8):
            c2(j).wait_recv()
        total = qc[yz]
        for j in range(1, 8):
            total = total + s2c[j]
        tc[...] = total

    @pl.when(is_odd)
    def _():
        sum_c1()
        sum_c2()
        n_pair().start()
        n_cross().start()

    def weighted(tile):
        r = lax.broadcasted_iota(jnp.int32, (8, 128), 0)
        scale = jnp.zeros((8, 128), jnp.float32)
        for q in range(4):
            scale = jnp.where(r == q, coupling[4 * dom + q], scale)
        return (scale * tile).astype(jnp.bfloat16).astype(jnp.float32)

    def outer(left, right):
        return lax.dot_general(
            left, right, (((0,), (0,)), ((), ())),
            precision=lax.Precision.HIGHEST, preferred_element_type=jnp.float32,
        )

    def f1(j):
        return remote(rr.at[lax.rem(xx + j, 4)], s1.at[j], f1_s.at[j], f1_r.at[j], band, x_peer(j))

    def f2_own(j):
        return remote(qq.at[0, lax.rem(yz + j, 8)], s2.at[j], f2_s.at[j], f2_r.at[j], band, yz_peer(j))

    def f2_cross(j):
        return remote(qq.at[1, lax.rem(yz + j, 8)], s2.at[j], f2_s.at[8 + j], f2_r.at[j], cross, yz_peer(j))

    @pl.when(is_even)
    def _():
        for k in (0, 2, 4, 6):
            halo(k).wait_recv()
        local_rows(64, 128)
        sum_c1()
        acc[...] = jnp.zeros_like(acc)

        @pl.loop(0, PARTS)
        def _(k):
            to_pair(k).wait_recv()
            to_cross(k).wait_recv()
            x = plane_of(k)
            first = lax.rem(k // 2, 2) * CHUNK

            @pl.loop(0, CHUNK // 4)
            def _(q):
                part = acc[...]
                for r in range(4):
                    y = first + q * 4 + r
                    left = jnp.concatenate([ext[x + 2, y], img[x, y]], axis=0)
                    part = part + dot_rows(left, other[x, y])
                acc[...] = part

        sum_c2()
        n_pair().wait_recv()
        n_cross().wait_recv()
        mine = tc[...]
        acc[128:256, 0:128] += outer(mine, weighted(nb[0]))
        acc[128:256, 128:256] += outer(weighted(mine), nb[1])
        acc[0:128, 128:256] = acc[0:128, 128:256].T
        acc[128:256, 128:256] = acc[128:256, 128:256].T
        for d in range(32):
            for half in range(2):
                cols = slice(128 * half, 128 * half + 128)
                rr[d % 4, half, d // 4, 0:4, :] = acc[4 * d:4 * d + 4, cols]
                rr[d % 4, half, d // 4, 4:8, :] = acc[128 + 4 * d:128 + 4 * d + 4, cols]
        for j in (1, 2, 3):
            f1(j).start()
        for j in (1, 2, 3):
            f1(j).wait_recv()
        qq[...] = (rr[xx] + s1[1]) + (s1[2] + s1[3])
        for j in range(8):
            f2_cross(j).start()
        for j in range(1, 8):
            f2_own(j).start()
        for j in range(1, 8):
            f2_own(j).wait_recv()
        s2[0] = qq[0, yz]

    @pl.when(is_odd)
    def _():
        for j in range(8):
            f2_cross(j).wait_recv()

    total = s2[0]
    for j in range(1, 8):
        total = total + s2[j]
    lane = lax.broadcasted_iota(jnp.int32, (8, 128), 1)
    block = dom // 16
    mask = jnp.where(lane < 64, pattern[block, 0], pattern[block, 1]).astype(jnp.float32)
    total = total * mask
    corr_out[...] = total[0:4]
    ham_out[...] = total[4:8]

    for j in (1, 2, 3):
        c1(j).wait_send()
    for j in range(1, 8):
        c2(j).wait_send()

    @pl.when(is_even)
    def _():
        for k in range(PARTS):
            halo(k).wait_send()
        for j in (1, 2, 3):
            f1(j).wait_send()
        for j in range(8):
            f2_cross(j).wait_send()
        for j in range(1, 8):
            f2_own(j).wait_send()

    @pl.when(is_odd)
    def _():
        for k in range(PARTS):
            to_pair(k).wait_send()
            to_cross(k).wait_send()
        n_pair().wait_send()
        n_cross().wait_send()


def on_device(orbitals, potential, projectors, coupling, pattern):
    f32, bf16 = jnp.float32, jnp.bfloat16
    dma = lambda n: pltpu.SemaphoreType.DMA((n,))
    hbm = pl.BlockSpec(memory_space=pl.ANY)
    vmem = pl.BlockSpec(memory_space=pltpu.VMEM)
    smem = pl.BlockSpec(memory_space=pltpu.SMEM)
    return tuple(pl.pallas_call(
        kernel,
        out_shape=[jax.ShapeDtypeStruct((4, 128), f32)] * 2,
        in_specs=[hbm, hbm, vmem, smem, smem],
        out_specs=[vmem, vmem],
        scratch_shapes=[
            pltpu.VMEM((2, 128, CHUNK, 256), bf16),
            pltpu.VMEM((2, 128, CHUNK, 256), bf16),
            pltpu.VMEM((CHUNK, 128, 256), bf16),
            pltpu.VMEM((PLANES + 4, 32, 128, 256), bf16),
            pltpu.VMEM((PLANES, 32, 128, 256), bf16),
            pltpu.VMEM((PLANES, 32, 256, 256), bf16),
            pltpu.VMEM((256, 256), bf16),
            pltpu.VMEM((128, 128), f32),
            pltpu.VMEM((256, 256), f32),
            pltpu.VMEM((4, 8, 8, 128), f32),
            pltpu.VMEM((4, 8, 8, 128), f32),
            pltpu.VMEM((8, 8, 128), f32),
            pltpu.VMEM((8, 8, 128), f32),
            pltpu.VMEM((8, 128), f32),
            pltpu.VMEM((2, 8, 128), f32),
            pltpu.VMEM((4, 2, 8, 8, 128), f32),
            pltpu.VMEM((4, 2, 8, 8, 128), f32),
            pltpu.VMEM((2, 8, 8, 128), f32),
            pltpu.VMEM((8, 8, 128), f32),
            dma(2), dma(2), dma(8), dma(8), dma(8), dma(8), dma(8), dma(8),
            dma(4), dma(4), dma(8), dma(8), dma(2), dma(2), dma(4), dma(4), dma(16), dma(8),
        ],
        compiler_params=pltpu.CompilerParams(
            collective_id=0, has_side_effects=True, vmem_limit_bytes=58 * 2**20,
        ),
    )(orbitals, projectors, potential, coupling, pattern))


def solution(mesh):
    return jax.shard_map(
        on_device,
        mesh=mesh,
        in_specs=(
            P("band", "dom", None, None),
            P("dom", None, None),
            P(None, "dom", None, None),
            P(),
            P("band", None),
        ),
        out_specs=(P(("band", "dom"), None), P(("band", "dom"), None)),
        check_vma=False,
    )
```

```python
import functools

import jax
import jax.numpy as jnp
from jax import lax
from jax.experimental import pallas as pl
from jax.experimental.pallas import tpu as pltpu
from jax.sharding import PartitionSpec as P

W_CENTER = 90.0
W_NEAR = -16.0
W_FAR = 1.0
W_SCALE = 1.0 / 24.0

MESH = pl.DeviceIdType.MESH
CHUNK = 16
PLANES = 4
PARTS = 8


def dot_rows(left, right):
    return lax.dot_general(left, right, (((1,), (1,)), ((), ())), preferred_element_type=jnp.float32)


def kernel(
    orb_hbm, proj_hbm, pot, coupling, pattern, corr_out, ham_out,
    nat, pnat, pt, ext, img, other, circ, coef, acc,
    rc, s1c, qc, s2c, tc, nb, rr, s1, qq, s2,
    in_sem, pin_sem, halo_s, halo_r, pair_s, pair_r, cross_s, cross_r,
    c1_s, c1_r, c2_s, c2_r, n_s, n_r, f1_s, f1_r, f2_s, f2_r, via_r, via_s,
):
    band = lax.axis_index("band")
    dom = lax.axis_index("dom")
    core = lax.rem(band, 2)
    zh = band // 2
    yz = dom // 4
    xx = lax.rem(dom, 4)
    partner = zh * 2 + (1 - core)
    cross = (1 - zh) * 2 + (1 - core)
    other_yz = yz + 1 - 2 * lax.rem(yz, 2)
    row_end = (lax.rem(other_yz * 4 + 31, 32), lax.rem(other_yz * 4 + 4, 32))
    is_even = core == 0
    is_odd = core == 1

    def x_peer(j):
        return yz * 4 + lax.rem(xx + j, 4)

    def yz_peer(j):
        return lax.rem(yz + j, 8) * 4 + xx

    def remote(src, dst, ssem, rsem, to_band, to_dom):
        return pltpu.make_async_remote_copy(
            src_ref=src, dst_ref=dst, send_sem=ssem, recv_sem=rsem,
            device_id=(to_band, to_dom), device_id_type=MESH,
        )

    def plane_of(k):
        return lax.rem(k, 2) * 2 + k // 4

    def rows_of(k):
        return pl.ds(pl.multiple_of(lax.rem(k // 2, 2) * CHUNK, CHUNK), CHUNK)

    def load(src, dst, sem, k):
        return pltpu.make_async_copy(src.at[:, plane_of(k), rows_of(k), :], dst.at[lax.rem(k, 2)], sem.at[lax.rem(k, 2)])

    def own(k):
        return ext.at[plane_of(k) + 2, rows_of(k)]

    def halo(k):
        side = lax.rem(k, 2)
        to_dom = lax.rem(dom + 31 + 2 * side, 32)
        return remote(own(k), ext.at[plane_of(k) + 6 - 8 * side, rows_of(k)], halo_s.at[k], halo_r.at[k], band, to_dom)

    def to_via(k):
        side = lax.rem(k, 2)
        c = k // 2
        column = c + side * (3 - 2 * c)
        dst = ext.at[6 - 6 * side, pl.ds(0, CHUNK)]
        return remote(own(k), dst, halo_s.at[k], via_r.at[side], partner, other_yz * 4 + column)

    def via_in(side):
        dst = ext.at[6 - 6 * side, pl.ds(0, CHUNK)]
        return remote(dst, dst, via_s.at[side], via_r.at[side], partner, row_end[side])

    def via(side):
        k = 2 * xx + side * (7 - 4 * xx)
        src = ext.at[6 - 6 * side, pl.ds(0, CHUNK)]
        dst = ext.at[plane_of(k) + 6 - 8 * side, rows_of(k)]
        return remote(src, dst, via_s.at[side], halo_r.at[k], partner, row_end[side])

    def to_pair(k):
        return remote(own(k), other.at[plane_of(k), rows_of(k), pl.ds(0, 128)], pair_s.at[k], pair_r.at[k], partner, dom)

    def to_cross(k):
        return remote(own(k), other.at[plane_of(k), rows_of(k), pl.ds(128, 128)], cross_s.at[k], cross_r.at[k], cross, dom)

    load(orb_hbm, nat, in_sem, 0).start()
    load(proj_hbm, pnat, pin_sem, 0).start()

    barrier = pltpu.get_barrier_semaphore()
    peers = [(band, x_peer(j)) for j in (1, 2, 3)]
    peers += [(band, yz_peer(j)) for j in range(1, 8)]
    peers += [(cross, yz_peer(j)) for j in range(8)]
    peers += [(partner, dom), (band, lax.rem(dom + 1, 32)), (band, lax.rem(dom + 31, 32))]
    for peer in peers:
        pl.semaphore_signal(barrier, inc=1, device_id=peer, device_id_type=MESH)

    def greet(peer):
        pl.semaphore_signal(barrier, inc=1, device_id=peer, device_id_type=MESH)

    @pl.when(is_odd)
    def _():
        for end in (other_yz * 4, other_yz * 4 + 3) + row_end:
            greet((partner, end))

    @pl.when(is_even & (xx == 0))
    def _():
        for j in range(4):
            greet((partner, other_yz * 4 + j))
            back = lax.rem(yz + 7, 8)
            greet((partner, (back + 1 - 2 * lax.rem(back, 2)) * 4 + j))

    @pl.when(is_even & (xx == 3))
    def _():
        for j in range(4):
            greet((partner, other_yz * 4 + j))
            ahead = lax.rem(yz + 1, 8)
            greet((partner, (ahead + 1 - 2 * lax.rem(ahead, 2)) * 4 + j))

    row = lax.broadcasted_iota(jnp.int32, (256, 256), 0)
    col = lax.broadcasted_iota(jnp.int32, (256, 256), 1)
    gap = (row - col) & 255
    near_z = (gap == 1) | (gap == 255)
    far_z = (gap == 2) | (gap == 254)
    circ[...] = jnp.where(gap == 0, W_CENTER, jnp.where(near_z, W_NEAR, jnp.where(far_z, W_FAR, 0.0))).astype(jnp.bfloat16)
    coef[...] = jnp.zeros_like(coef)
    rc[...] = jnp.zeros_like(rc)

    row_ends = (xx == 0) | (xx == 3)

    @pl.when(is_odd)
    def _():
        pl.semaphore_wait(barrier, len(peers) + 4)

    @pl.when(is_even & row_ends)
    def _():
        pl.semaphore_wait(barrier, len(peers) + 8)

    @pl.when(is_even & jnp.logical_not(row_ends))
    def _():
        pl.semaphore_wait(barrier, len(peers))

    @pl.loop(0, PARTS)
    def _(k):
        slot = lax.rem(k, 2)

        @pl.when(k + 1 < PARTS)
        def _():
            load(orb_hbm, nat, in_sem, k + 1).start()
            load(proj_hbm, pnat, pin_sem, k + 1).start()

        load(orb_hbm, nat, in_sem, k).wait()
        px = plane_of(k) + 2
        rows = rows_of(k)

        @pl.loop(0, 8)
        def _(q):
            r = pl.ds(pl.multiple_of(q * 16, 16), 16)
            ext[px, rows, r, :] = jnp.swapaxes(nat[slot, r], 0, 1)

        @pl.when(is_even)
        def _():
            at_end = ((xx == 0) & (slot == 0)) | ((xx == 3) & (slot == 1))
            through = at_end & (k < 6)

            @pl.when(through)
            def _():
                to_via(k).start()

            @pl.when(jnp.logical_not(through))
            def _():
                halo(k).start()

        @pl.when(is_odd)
        def _():
            to_cross(k).start()
            to_pair(k).start()

        load(proj_hbm, pnat, pin_sem, k).wait()

        @pl.loop(0, 8)
        def _(q):
            r = pl.ds(pl.multiple_of(q * 16, 16), 16)
            pt[:, r, :] = jnp.swapaxes(pnat[slot, r], 0, 1)

        first = lax.rem(k // 2, 2) * CHUNK
        part = coef[...]
        for r in range(CHUNK):
            part = part + dot_rows(pt[r], ext[px, first + r])
        coef[...] = part

    for d in range(32):
        rc[d % 4, d // 4, 0:4, :] = coef[4 * d:4 * d + 4, :]

    def c1(j):
        return remote(rc.at[lax.rem(xx + j, 4)], s1c.at[j], c1_s.at[j], c1_r.at[j], band, x_peer(j))

    def c2(j):
        return remote(qc.at[lax.rem(yz + j, 8)], s2c.at[j], c2_s.at[j], c2_r.at[j], band, yz_peer(j))

    def n_pair():
        return remote(tc, nb.at[0], n_s.at[0], n_r.at[0], partner, dom)

    def n_cross():
        return remote(tc, nb.at[1], n_s.at[1], n_r.at[1], cross, dom)

    for j in (1, 2, 3):
        c1(j).start()

    def local_rows(start, stop):
        def body(k, carry):
            x = k // 32
            y = lax.rem(k, 32)

            def at(dx, dy):
                return ext[x + 2 + dx, lax.rem(y + 32 + dy, 32)].astype(jnp.float32)

            center = ext[x + 2, y]
            own_z = jnp.dot(center, circ[...], preferred_element_type=jnp.float32)
            near = (at(-1, 0) + at(1, 0)) + (at(0, -1) + at(0, 1))
            far = (at(-2, 0) + at(2, 0)) + (at(0, -2) + at(0, 2))
            kinetic = (own_z + W_NEAR * near + far) * W_SCALE
            img[x, y] = (kinetic + pot[x, pl.ds(y, 1), :] * center.astype(jnp.float32)).astype(jnp.bfloat16)
            return carry

        lax.fori_loop(start, stop, body, 0)

    @pl.when(is_even)
    def _():
        for k in (1, 3, 5, 7):
            halo(k).wait_recv()
        local_rows(0, 64)

    def sum_c1():
        for j in (1, 2, 3):
            c1(j).wait_recv()
        qc[...] = (rc[xx] + s1c[1]) + (s1c[2] + s1c[3])
        for j in range(1, 8):
            c2(j).start()

    def sum_c2():
        for j in range(1, 8):
            c2(j).wait_recv()
        total = qc[yz]
        for j in range(1, 8):
            total = total + s2c[j]
        tc[...] = total

    @pl.when(is_odd & (xx != 3))
    def _():
        via_in(0).wait_recv()
        via(0).start()

    @pl.when(is_odd & (xx != 0))
    def _():
        via_in(1).wait_recv()
        via(1).start()

    @pl.when(is_odd)
    def _():
        sum_c1()
        sum_c2()
        n_pair().start()
        n_cross().start()

    def weighted(tile):
        r = lax.broadcasted_iota(jnp.int32, (8, 128), 0)
        scale = jnp.zeros((8, 128), jnp.float32)
        for q in range(4):
            scale = jnp.where(r == q, coupling[4 * dom + q], scale)
        return (scale * tile).astype(jnp.bfloat16).astype(jnp.float32)

    def outer(left, right):
        return lax.dot_general(
            left, right, (((0,), (0,)), ((), ())),
            precision=lax.Precision.HIGHEST, preferred_element_type=jnp.float32,
        )

    def f1(j):
        return remote(rr.at[lax.rem(xx + j, 4)], s1.at[j], f1_s.at[j], f1_r.at[j], band, x_peer(j))

    def f2_own(j):
        return remote(qq.at[0, lax.rem(yz + j, 8)], s2.at[j], f2_s.at[j], f2_r.at[j], band, yz_peer(j))

    def f2_cross(j):
        return remote(qq.at[1, lax.rem(yz + j, 8)], s2.at[j], f2_s.at[8 + j], f2_r.at[j], cross, yz_peer(j))

    @pl.when(is_even)
    def _():
        for k in (0, 2, 4, 6):
            halo(k).wait_recv()
        local_rows(64, 128)
        sum_c1()
        acc[...] = jnp.zeros_like(acc)

        @pl.loop(0, PARTS)
        def _(k):
            to_pair(k).wait_recv()
            to_cross(k).wait_recv()
            x = plane_of(k)
            first = lax.rem(k // 2, 2) * CHUNK

            @pl.loop(0, CHUNK // 4)
            def _(q):
                part = acc[...]
                for r in range(4):
                    y = first + q * 4 + r
                    left = jnp.concatenate([ext[x + 2, y], img[x, y]], axis=0)
                    part = part + dot_rows(left, other[x, y])
                acc[...] = part

        sum_c2()
        n_pair().wait_recv()
        n_cross().wait_recv()
        mine = tc[...]
        acc[128:256, 0:128] += outer(mine, weighted(nb[0]))
        acc[128:256, 128:256] += outer(weighted(mine), nb[1])
        acc[0:128, 128:256] = acc[0:128, 128:256].T
        acc[128:256, 128:256] = acc[128:256, 128:256].T
        for d in range(32):
            for half in range(2):
                cols = slice(128 * half, 128 * half + 128)
                rr[d % 4, half, d // 4, 0:4, :] = acc[4 * d:4 * d + 4, cols]
                rr[d % 4, half, d // 4, 4:8, :] = acc[128 + 4 * d:128 + 4 * d + 4, cols]
        for j in (1, 2, 3):
            f1(j).start()
        for j in (1, 2, 3):
            f1(j).wait_recv()
        qq[...] = (rr[xx] + s1[1]) + (s1[2] + s1[3])
        for j in range(8):
            f2_cross(j).start()
        for j in range(1, 8):
            f2_own(j).start()
        for j in range(1, 8):
            f2_own(j).wait_recv()
        s2[0] = qq[0, yz]

    @pl.when(is_odd)
    def _():
        for j in range(8):
            f2_cross(j).wait_recv()

    total = s2[0]
    for j in range(1, 8):
        total = total + s2[j]
    lane = lax.broadcasted_iota(jnp.int32, (8, 128), 1)
    block = dom // 16
    mask = jnp.where(lane < 64, pattern[block, 0], pattern[block, 1]).astype(jnp.float32)
    total = total * mask
    corr_out[...] = total[0:4]
    ham_out[...] = total[4:8]

    for j in (1, 2, 3):
        c1(j).wait_send()
    for j in range(1, 8):
        c2(j).wait_send()

    @pl.when(is_even)
    def _():
        for k in range(PARTS):
            halo(k).wait_send()
        for j in (1, 2, 3):
            f1(j).wait_send()
        for j in range(8):
            f2_cross(j).wait_send()
        for j in range(1, 8):
            f2_own(j).wait_send()

    @pl.when(is_odd)
    def _():
        for k in range(PARTS):
            to_pair(k).wait_send()
            to_cross(k).wait_send()
        n_pair().wait_send()
        n_cross().wait_send()

    @pl.when(is_odd & (xx != 3))
    def _():
        via(0).wait_send()

    @pl.when(is_odd & (xx != 0))
    def _():
        via(1).wait_send()


def on_device(orbitals, potential, projectors, coupling, pattern):
    f32, bf16 = jnp.float32, jnp.bfloat16
    dma = lambda n: pltpu.SemaphoreType.DMA((n,))
    hbm = pl.BlockSpec(memory_space=pl.ANY)
    vmem = pl.BlockSpec(memory_space=pltpu.VMEM)
    smem = pl.BlockSpec(memory_space=pltpu.SMEM)
    return tuple(pl.pallas_call(
        kernel,
        out_shape=[jax.ShapeDtypeStruct((4, 128), f32)] * 2,
        in_specs=[hbm, hbm, vmem, smem, smem],
        out_specs=[vmem, vmem],
        scratch_shapes=[
            pltpu.VMEM((2, 128, CHUNK, 256), bf16),
            pltpu.VMEM((2, 128, CHUNK, 256), bf16),
            pltpu.VMEM((CHUNK, 128, 256), bf16),
            pltpu.VMEM((PLANES + 4, 32, 128, 256), bf16),
            pltpu.VMEM((PLANES, 32, 128, 256), bf16),
            pltpu.VMEM((PLANES, 32, 256, 256), bf16),
            pltpu.VMEM((256, 256), bf16),
            pltpu.VMEM((128, 128), f32),
            pltpu.VMEM((256, 256), f32),
            pltpu.VMEM((4, 8, 8, 128), f32),
            pltpu.VMEM((4, 8, 8, 128), f32),
            pltpu.VMEM((8, 8, 128), f32),
            pltpu.VMEM((8, 8, 128), f32),
            pltpu.VMEM((8, 128), f32),
            pltpu.VMEM((2, 8, 128), f32),
            pltpu.VMEM((4, 2, 8, 8, 128), f32),
            pltpu.VMEM((4, 2, 8, 8, 128), f32),
            pltpu.VMEM((2, 8, 8, 128), f32),
            pltpu.VMEM((8, 8, 128), f32),
            dma(2), dma(2), dma(8), dma(8), dma(8), dma(8), dma(8), dma(8),
            dma(4), dma(4), dma(8), dma(8), dma(2), dma(2), dma(4), dma(4), dma(16), dma(8), dma(2), dma(2),
        ],
        compiler_params=pltpu.CompilerParams(
            collective_id=0, has_side_effects=True, vmem_limit_bytes=58 * 2**20,
        ),
    )(orbitals, projectors, potential, coupling, pattern))


def solution(mesh):
    return jax.shard_map(
        on_device,
        mesh=mesh,
        in_specs=(
            P("band", "dom", None, None),
            P("dom", None, None),
            P(None, "dom", None, None),
            P(),
            P("band", None),
        ),
        out_specs=(P(("band", "dom"), None), P(("band", "dom"), None)),
        check_vma=False,
    )
```

```python
import functools

import jax
import jax.numpy as jnp
from jax import lax
from jax.experimental import pallas as pl
from jax.experimental.pallas import tpu as pltpu
from jax.sharding import PartitionSpec as P

W_CENTER = 90.0
W_NEAR = -16.0
W_FAR = 1.0
W_SCALE = 1.0 / 24.0

MESH = pl.DeviceIdType.MESH

HANDED_ON = {0: ((4, False),), 1: ((0, False), (1, True)), 2: ((2, True), (3, False)), 3: ((7, False),)}
CHUNK = 16
PLANES = 4
PARTS = 8


def dot_rows(left, right):
    return lax.dot_general(left, right, (((1,), (1,)), ((), ())), preferred_element_type=jnp.float32)


def kernel(
    orb_hbm, proj_hbm, pot, coupling, pattern, corr_out, ham_out,
    nat, pnat, pt, ext, far_in, img, other, circ, coef, acc, acc_twin, twin_in,
    rc, s1c, qc, s2c, tc, nb, rr, s1, qq, s2,
    in_sem, pin_sem, halo_s, halo_r, pair_s, pair_r, cross_s, cross_r,
    c1_s, c1_r, c2_s, c2_r, n_s, n_r, f1_s, f1_r, f2_s, f2_r, via_r, via_s, t_s, t_r,
):
    band = lax.axis_index("band")
    dom = lax.axis_index("dom")
    core = lax.rem(band, 2)
    zh = band // 2
    yz = dom // 4
    zl = lax.rem(yz, 2)
    xx = lax.rem(dom, 4)
    partner = zh * 2 + (1 - core)
    cross = (1 - zh) * 2 + (1 - core)
    twin = (1 - zh) * 2 + core
    other_yz = yz + 1 - 2 * lax.rem(yz, 2)
    row_end = (lax.rem(other_yz * 4 + 31, 32), lax.rem(other_yz * 4 + 4, 32))
    is_even = core == 0
    is_odd = core == 1

    def x_peer(j):
        return yz * 4 + lax.rem(xx + j, 4)

    def yz_peer(j):
        return lax.rem(yz + j, 8) * 4 + xx

    def remote(src, dst, ssem, rsem, to_band, to_dom):
        return pltpu.make_async_remote_copy(
            src_ref=src, dst_ref=dst, send_sem=ssem, recv_sem=rsem,
            device_id=(to_band, to_dom), device_id_type=MESH,
        )

    def plane_of(k):
        return lax.rem(k, 2) * 2 + k // 4

    def first_row(k):
        return (1 - lax.rem(k // 2, 2)) * CHUNK

    def rows_of(k):
        return pl.ds(pl.multiple_of(first_row(k), CHUNK), CHUNK)

    def pair_order(i):
        i = lax.rem(i + 4 * (1 - zl), PARTS)
        return lax.rem(3 * (i // 2), 4) + 4 * lax.rem(i, 2)

    def own_order(i):
        return i + core * (pair_order(i) - i)

    def load(src, dst, sem, i):
        k, slot = own_order(i), lax.rem(i, 2)
        return pltpu.make_async_copy(src.at[:, plane_of(k), rows_of(k), :], dst.at[slot], sem.at[slot])

    def own(k):
        return ext.at[plane_of(k) + 2, rows_of(k)]

    def halo(k):
        side = lax.rem(k, 2)
        to_dom = lax.rem(dom + 31 + 2 * side, 32)
        return remote(own(k), ext.at[plane_of(k) + 6 - 8 * side, rows_of(k)], halo_s.at[k], halo_r.at[k], band, to_dom)

    def other_odd(flag, z):
        far = int(flag) + z - 2 * int(flag) * z
        return partner + far * (cross - partner)

    def to_via(k, flag, column):
        dst = ext.at[6 - 6 * (k % 2), pl.ds(0, CHUNK)]
        return remote(own(k), dst, halo_s.at[k], via_r.at[k % 2], other_odd(flag, zl), other_yz * 4 + column)

    def to_twin(k):
        to_dom = lax.rem(dom + 31 + 2 * lax.rem(k, 2), 32)
        return remote(own(k), far_in.at[k // 4], halo_s.at[k], halo_r.at[k], twin, to_dom)

    def via_in(k):
        dst = ext.at[6 - 6 * (k % 2), pl.ds(0, CHUNK)]
        return remote(dst, dst, via_s.at[k % 2], via_r.at[k % 2], partner, row_end[0])

    def via(k, far):
        side = k % 2
        src = ext.at[6 - 6 * side, pl.ds(0, CHUNK)]
        dst = far_in.at[k // 4] if far else ext.at[plane_of(k) + 6 - 8 * side, rows_of(k)]
        return remote(src, dst, via_s.at[side], halo_r.at[k], partner, row_end[side])

    def twin_sum():
        return remote(acc_twin, twin_in, t_s.at[0], t_r.at[0], twin, dom)

    def to_pair(k):
        return remote(own(k), other.at[plane_of(k), rows_of(k), pl.ds(0, 128)], pair_s.at[k], pair_r.at[k], partner, dom)

    def to_cross(k):
        return remote(own(k), other.at[plane_of(k), rows_of(k), pl.ds(128, 128)], cross_s.at[k], cross_r.at[k], cross, dom)

    load(orb_hbm, nat, in_sem, 0).start()
    load(proj_hbm, pnat, pin_sem, 0).start()

    barrier = pltpu.get_barrier_semaphore()
    peers = [(band, x_peer(j)) for j in (1, 2, 3)]
    peers += [(band, yz_peer(j)) for j in range(1, 8)]
    peers += [(cross, yz_peer(j)) for j in range(8)]
    peers += [(partner, dom), (twin, dom)]
    peers += [(b, lax.rem(dom + step, 32)) for b in (band, twin) for step in (1, 31)]
    for peer in peers:
        pl.semaphore_signal(barrier, inc=1, device_id=peer, device_id_type=MESH)

    def greet(peer):
        pl.semaphore_signal(barrier, inc=1, device_id=peer, device_id_type=MESH)

    up_end = is_even & (xx == 3)
    down_end = is_even & (xx == 0)
    ahead = lax.rem(yz + 1, 8)
    back = lax.rem(yz + 7, 8)

    for column, chunks in HANDED_ON.items():

        @pl.when(is_odd & (xx == column))
        def _():
            for k, flag in chunks:
                greet((other_odd(flag, 1 - zl), other_yz * 4 + 3 * (k % 2)))
                greet((partner, row_end[k % 2]))

    for end, side, last in ((up_end, 1, ahead), (down_end, 0, back)):

        @pl.when(end)
        def _():
            for column, chunks in HANDED_ON.items():
                for k, flag in chunks:
                    if k % 2 == side:
                        greet((other_odd(flag, zl), other_yz * 4 + column))
                    else:
                        greet((partner, (last + 1 - 2 * lax.rem(last, 2)) * 4 + column))

    row = lax.broadcasted_iota(jnp.int32, (256, 256), 0)
    col = lax.broadcasted_iota(jnp.int32, (256, 256), 1)
    gap = (row - col) & 255
    near_z = (gap == 1) | (gap == 255)
    far_z = (gap == 2) | (gap == 254)
    circ[...] = jnp.where(gap == 0, W_CENTER, jnp.where(near_z, W_NEAR, jnp.where(far_z, W_FAR, 0.0))).astype(jnp.bfloat16)
    coef[...] = jnp.zeros_like(coef)
    rc[...] = jnp.zeros_like(rc)

    at_end = up_end | down_end
    edge = (xx == 0) | (xx == 3)
    kinds = (
        (at_end, 6),
        (is_odd & edge, 2),
        (is_odd & jnp.logical_not(edge), 4),
        (is_even & jnp.logical_not(edge), 0),
    )
    for kind, count in kinds:

        @pl.when(kind)
        def _():
            pl.semaphore_wait(barrier, len(peers) + count)

    @pl.when(down_end)
    def _():
        ext[0:2, pl.ds(pl.multiple_of(CHUNK * zl, CHUNK), CHUNK), :, :] = jnp.zeros((2, CHUNK, 128, 256), jnp.bfloat16)

    @pl.when(up_end)
    def _():
        ext[6:8, pl.ds(pl.multiple_of(CHUNK * (1 - zl), CHUNK), CHUNK), :, :] = jnp.zeros((2, CHUNK, 128, 256), jnp.bfloat16)

    @pl.loop(0, PARTS)
    def _(i):
        slot = lax.rem(i, 2)
        k = own_order(i)

        @pl.when(i + 1 < PARTS)
        def _():
            load(orb_hbm, nat, in_sem, i + 1).start()
            load(proj_hbm, pnat, pin_sem, i + 1).start()

        load(orb_hbm, nat, in_sem, i).wait()
        px = plane_of(k) + 2
        rows = rows_of(k)

        @pl.loop(0, 8)
        def _(q):
            r = pl.ds(pl.multiple_of(q * 16, 16), 16)
            ext[px, rows, r, :] = jnp.swapaxes(nat[slot, r], 0, 1)

        @pl.when(is_even)
        def _():
            for column, chunks in HANDED_ON.items():
                for c, flag in chunks:

                    @pl.when((up_end if c % 2 else down_end) & (k == c))
                    def _():
                        to_via(c, flag, column).start()

            straight = (down_end & (k == 6)) | (up_end & (k == 5))
            across = (down_end & (slot == 0)) | (up_end & (slot == 1))

            @pl.when(straight & (zl == 0))
            def _():
                to_twin(k).start()

            @pl.when(jnp.logical_not(across) | (straight & (zl == 1)))
            def _():
                halo(k).start()

        @pl.when(is_odd)
        def _():
            to_cross(k).start()
            to_pair(k).start()

        load(proj_hbm, pnat, pin_sem, i).wait()

        @pl.loop(0, 8)
        def _(q):
            r = pl.ds(pl.multiple_of(q * 16, 16), 16)
            pt[:, r, :] = jnp.swapaxes(pnat[slot, r], 0, 1)

        first = first_row(k)
        part = coef[...]
        for r in range(CHUNK):
            part = part + dot_rows(pt[r], ext[px, first + r])
        coef[...] = part

    for d in range(32):
        rc[d % 4, d // 4, 0:4, :] = coef[4 * d:4 * d + 4, :]

    def c1(j):
        return remote(rc.at[lax.rem(xx + j, 4)], s1c.at[j], c1_s.at[j], c1_r.at[j], band, x_peer(j))

    def c2(j):
        return remote(qc.at[lax.rem(yz + j, 8)], s2c.at[j], c2_s.at[j], c2_r.at[j], band, yz_peer(j))

    def n_pair():
        return remote(tc, nb.at[0], n_s.at[0], n_r.at[0], partner, dom)

    def n_cross():
        return remote(tc, nb.at[1], n_s.at[1], n_r.at[1], cross, dom)

    for j in (1, 2, 3):
        c1(j).start()

    def local_rows(start, stop):
        def body(k, carry):
            x = k // 32
            y = lax.rem(k, 32)

            def at(dx, dy):
                return ext[x + 2 + dx, lax.rem(y + 32 + dy, 32)].astype(jnp.float32)

            center = ext[x + 2, y]
            own_z = jnp.dot(center, circ[...], preferred_element_type=jnp.float32)
            near = (at(-1, 0) + at(1, 0)) + (at(0, -1) + at(0, 1))
            far = (at(-2, 0) + at(2, 0)) + (at(0, -2) + at(0, 2))
            kinetic = (own_z + W_NEAR * near + far) * W_SCALE
            img[x, y] = (kinetic + pot[x, pl.ds(y, 1), :] * center.astype(jnp.float32)).astype(jnp.bfloat16)
            return carry

        lax.fori_loop(start, stop, body, 0)

    def first_planes():
        for k in (1, 3, 5, 7):
            halo(k).wait_recv()
        local_rows(0, 64)

    def last_planes():
        for k in (0, 2, 4, 6):
            halo(k).wait_recv()
        local_rows(64, 128)

    @pl.when(down_end)
    def _():
        last_planes()

    @pl.when(is_even & (xx != 0))
    def _():
        first_planes()

    def sum_c1():
        for j in (1, 2, 3):
            c1(j).wait_recv()
        qc[...] = (rc[xx] + s1c[1]) + (s1c[2] + s1c[3])
        for j in range(1, 8):
            c2(j).start()

    def sum_c2():
        for j in range(1, 8):
            c2(j).wait_recv()
        total = qc[yz]
        for j in range(1, 8):
            total = total + s2c[j]
        tc[...] = total

    for column, chunks in HANDED_ON.items():

        for z in range(2):

            @pl.when(is_odd & (xx == column) & (zl == z))
            def _():
                for k, flag in chunks:
                    via_in(k).wait_recv()
                    via(k, flag == (z == 1)).start()

    @pl.when(is_odd)
    def _():
        sum_c1()
        sum_c2()
        n_pair().start()
        n_cross().start()

    def weighted(tile):
        r = lax.broadcasted_iota(jnp.int32, (8, 128), 0)
        scale = jnp.zeros((8, 128), jnp.float32)
        for q in range(4):
            scale = jnp.where(r == q, coupling[4 * dom + q], scale)
        return (scale * tile).astype(jnp.bfloat16).astype(jnp.float32)

    def outer(left, right):
        return lax.dot_general(
            left, right, (((0,), (0,)), ((), ())),
            precision=lax.Precision.HIGHEST, preferred_element_type=jnp.float32,
        )

    def f1(j):
        return remote(rr.at[lax.rem(xx + j, 4)], s1.at[j], f1_s.at[j], f1_r.at[j], band, x_peer(j))

    def f2_own(j):
        return remote(qq.at[0, lax.rem(yz + j, 8)], s2.at[j], f2_s.at[j], f2_r.at[j], band, yz_peer(j))

    def f2_cross(j):
        return remote(qq.at[1, lax.rem(yz + j, 8)], s2.at[j], f2_s.at[8 + j], f2_r.at[j], cross, yz_peer(j))

    @pl.when(down_end)
    def _():
        first_planes()

    @pl.when(is_even & (xx != 0))
    def _():
        last_planes()

    @pl.when(is_even)
    def _():
        sum_c1()
        acc[...] = jnp.zeros_like(acc)

        def products(i):
            k = pair_order(i)
            to_pair(k).wait_recv()
            to_cross(k).wait_recv()
            x = plane_of(k)
            first = first_row(k)

            @pl.loop(0, CHUNK // 4)
            def _(q):
                part = acc[...]
                for r in range(4):
                    y = first + q * 4 + r
                    left = jnp.concatenate([ext[x + 2, y], img[x, y]], axis=0)
                    part = part + dot_rows(left, other[x, y])
                acc[...] = part

        pl.loop(0, 4)(products)

        def twin_products(first, outer_plane, inner_plane, near_at, far_at):
            acc_twin[...] = jnp.zeros_like(acc_twin)

            @pl.loop(0, CHUNK)
            def _(r):
                near = far_in[near_at, r].astype(jnp.float32)
                far = far_in[far_at, r].astype(jnp.float32)
                outer_part = ((W_NEAR * near + W_FAR * far) * W_SCALE).astype(jnp.bfloat16)
                inner_part = ((W_FAR * W_SCALE) * near).astype(jnp.bfloat16)
                acc_twin[...] += dot_rows(outer_part, other[outer_plane, first + r]) + dot_rows(
                    inner_part, other[inner_plane, first + r]
                )

            twin_sum().start()

        @pl.when(down_end)
        def _():
            twin_products(CHUNK * zl, 0, 1, 1, 0)

        @pl.when(up_end)
        def _():
            twin_products(CHUNK * (1 - zl), 3, 2, 0, 1)

        pl.loop(4, PARTS)(products)

        @pl.when(at_end)
        def _():
            twin_sum().wait_recv()
            acc[128:256, 0:128] += twin_in[:, 128:256]
            acc[128:256, 128:256] += twin_in[:, 0:128]

        sum_c2()
        n_pair().wait_recv()
        n_cross().wait_recv()
        mine = tc[...]
        acc[128:256, 0:128] += outer(mine, weighted(nb[0]))
        acc[128:256, 128:256] += outer(weighted(mine), nb[1])
        acc[0:128, 128:256] = acc[0:128, 128:256].T
        acc[128:256, 128:256] = acc[128:256, 128:256].T
        for d in range(32):
            for half in range(2):
                cols = slice(128 * half, 128 * half + 128)
                rr[d % 4, half, d // 4, 0:4, :] = acc[4 * d:4 * d + 4, cols]
                rr[d % 4, half, d // 4, 4:8, :] = acc[128 + 4 * d:128 + 4 * d + 4, cols]
        for j in (1, 2, 3):
            f1(j).start()
        for j in (1, 2, 3):
            f1(j).wait_recv()
        qq[...] = (rr[xx] + s1[1]) + (s1[2] + s1[3])
        for j in range(8):
            f2_cross(j).start()
        for j in range(1, 8):
            f2_own(j).start()
        for j in range(1, 8):
            f2_own(j).wait_recv()
        s2[0] = qq[0, yz]

    @pl.when(is_odd)
    def _():
        for j in range(8):
            f2_cross(j).wait_recv()

    total = s2[0]
    for j in range(1, 8):
        total = total + s2[j]
    lane = lax.broadcasted_iota(jnp.int32, (8, 128), 1)
    block = dom // 16
    mask = jnp.where(lane < 64, pattern[block, 0], pattern[block, 1]).astype(jnp.float32)
    total = total * mask
    corr_out[...] = total[0:4]
    ham_out[...] = total[4:8]

    for j in (1, 2, 3):
        c1(j).wait_send()
    for j in range(1, 8):
        c2(j).wait_send()

    @pl.when(is_even)
    def _():
        for k in range(PARTS):
            halo(k).wait_send()
        for j in (1, 2, 3):
            f1(j).wait_send()
        for j in range(8):
            f2_cross(j).wait_send()
        for j in range(1, 8):
            f2_own(j).wait_send()

    @pl.when(is_odd)
    def _():
        for k in range(PARTS):
            to_pair(k).wait_send()
            to_cross(k).wait_send()
        n_pair().wait_send()
        n_cross().wait_send()

    for column, chunks in HANDED_ON.items():

        @pl.when(is_odd & (xx == column))
        def _():
            for k, _flag in chunks:
                via(k, False).wait_send()

    @pl.when(at_end)
    def _():
        twin_sum().wait_send()


def on_device(orbitals, potential, projectors, coupling, pattern):
    f32, bf16 = jnp.float32, jnp.bfloat16
    dma = lambda n: pltpu.SemaphoreType.DMA((n,))
    hbm = pl.BlockSpec(memory_space=pl.ANY)
    vmem = pl.BlockSpec(memory_space=pltpu.VMEM)
    smem = pl.BlockSpec(memory_space=pltpu.SMEM)
    return tuple(pl.pallas_call(
        kernel,
        out_shape=[jax.ShapeDtypeStruct((4, 128), f32)] * 2,
        in_specs=[hbm, hbm, vmem, smem, smem],
        out_specs=[vmem, vmem],
        scratch_shapes=[
            pltpu.VMEM((2, 128, CHUNK, 256), bf16),
            pltpu.VMEM((2, 128, CHUNK, 256), bf16),
            pltpu.VMEM((CHUNK, 128, 256), bf16),
            pltpu.VMEM((PLANES + 4, 32, 128, 256), bf16),
            pltpu.VMEM((2, CHUNK, 128, 256), bf16),
            pltpu.VMEM((PLANES, 32, 128, 256), bf16),
            pltpu.VMEM((PLANES, 32, 256, 256), bf16),
            pltpu.VMEM((256, 256), bf16),
            pltpu.VMEM((128, 128), f32),
            pltpu.VMEM((256, 256), f32),
            pltpu.VMEM((128, 256), f32),
            pltpu.VMEM((128, 256), f32),
            pltpu.VMEM((4, 8, 8, 128), f32),
            pltpu.VMEM((4, 8, 8, 128), f32),
            pltpu.VMEM((8, 8, 128), f32),
            pltpu.VMEM((8, 8, 128), f32),
            pltpu.VMEM((8, 128), f32),
            pltpu.VMEM((2, 8, 128), f32),
            pltpu.VMEM((4, 2, 8, 8, 128), f32),
            pltpu.VMEM((4, 2, 8, 8, 128), f32),
            pltpu.VMEM((2, 8, 8, 128), f32),
            pltpu.VMEM((8, 8, 128), f32),
            dma(2), dma(2), dma(8), dma(8), dma(8), dma(8), dma(8), dma(8),
            dma(4), dma(4), dma(8), dma(8), dma(2), dma(2), dma(4), dma(4), dma(16), dma(8), dma(2), dma(2), dma(1), dma(1),
        ],
        compiler_params=pltpu.CompilerParams(
            collective_id=0, has_side_effects=True, vmem_limit_bytes=58 * 2**20,
        ),
    )(orbitals, projectors, potential, coupling, pattern))


def solution(mesh):
    return jax.shard_map(
        on_device,
        mesh=mesh,
        in_specs=(
            P("band", "dom", None, None),
            P("dom", None, None),
            P(None, "dom", None, None),
            P(),
            P("band", None),
        ),
        out_specs=(P(("band", "dom"), None), P(("band", "dom"), None)),
        check_vma=False,
    )
```

```python
import functools

import jax
import jax.numpy as jnp
from jax import lax
from jax.experimental import pallas as pl
from jax.experimental.pallas import tpu as pltpu
from jax.sharding import PartitionSpec as P

W_CENTER = 90.0
W_NEAR = -16.0
W_FAR = 1.0
W_SCALE = 1.0 / 24.0

MESH = pl.DeviceIdType.MESH

HANDED_ON = {0: ((4, False),), 1: ((0, False), (1, True)), 2: ((2, True), (3, False)), 3: ((7, False),)}
CHUNK = 16
PLANES = 4
PARTS = 8


def dot_rows(left, right):
    return lax.dot_general(left, right, (((1,), (1,)), ((), ())), preferred_element_type=jnp.float32)


def kernel(
    orb_hbm, proj_hbm, pot, coupling, pattern, corr_out, ham_out,
    nat, pnat, pt, ext, far_in, img, other, circ, coef, acc, acc_twin, twin_in,
    rc, s1c, qc, s2c, tc, nb, rr, s1, qq, s2,
    in_sem, pin_sem, halo_s, halo_r, pair_s, pair_r, cross_s, cross_r,
    c1_s, c1_r, c2_s, c2_r, n_s, n_r, f1_s, f1_r, f2_s, f2_r, via_r, via_s, t_s, t_r,
):
    band = lax.axis_index("band")
    dom = lax.axis_index("dom")
    core = lax.rem(band, 2)
    zh = band // 2
    yz = dom // 4
    zl = lax.rem(yz, 2)
    xx = lax.rem(dom, 4)
    partner = zh * 2 + (1 - core)
    cross = (1 - zh) * 2 + (1 - core)
    twin = (1 - zh) * 2 + core
    other_yz = yz + 1 - 2 * lax.rem(yz, 2)
    row_end = (lax.rem(other_yz * 4 + 31, 32), lax.rem(other_yz * 4 + 4, 32))
    is_even = core == 0
    is_odd = core == 1

    def x_peer(j):
        return yz * 4 + lax.rem(xx + j, 4)

    def yz_peer(j):
        return lax.rem(yz + j, 8) * 4 + xx

    def remote(src, dst, ssem, rsem, to_band, to_dom):
        return pltpu.make_async_remote_copy(
            src_ref=src, dst_ref=dst, send_sem=ssem, recv_sem=rsem,
            device_id=(to_band, to_dom), device_id_type=MESH,
        )

    def plane_of(k):
        return lax.rem(k, 2) * 2 + k // 4

    def first_row(k):
        return (1 - lax.rem(k // 2, 2)) * CHUNK

    def rows_of(k):
        return pl.ds(pl.multiple_of(first_row(k), CHUNK), CHUNK)

    def pair_order(i):
        i = lax.rem(i + 4 * (1 - zl), PARTS)
        return lax.rem(3 * (i // 2), 4) + 4 * lax.rem(i, 2)

    def own_order(i):
        return i + core * (pair_order(i) - i)

    def load(src, dst, sem, i):
        k, slot = own_order(i), lax.rem(i, 2)
        return pltpu.make_async_copy(src.at[:, plane_of(k), rows_of(k), :], dst.at[slot], sem.at[slot])

    def own(k):
        return ext.at[plane_of(k) + 2, rows_of(k)]

    def halo(k):
        side = lax.rem(k, 2)
        to_dom = lax.rem(dom + 31 + 2 * side, 32)
        return remote(own(k), ext.at[plane_of(k) + 6 - 8 * side, rows_of(k)], halo_s.at[k], halo_r.at[k], band, to_dom)

    def other_odd(flag, z):
        far = int(flag) + z - 2 * int(flag) * z
        return partner + far * (cross - partner)

    def to_via(k, flag, column):
        dst = ext.at[6 - 6 * (k % 2), pl.ds(0, CHUNK)]
        return remote(own(k), dst, halo_s.at[k], via_r.at[k % 2], other_odd(flag, zl), other_yz * 4 + column)

    def to_twin(k):
        to_dom = lax.rem(dom + 31 + 2 * lax.rem(k, 2), 32)
        return remote(own(k), far_in.at[k // 4], halo_s.at[k], halo_r.at[k], twin, to_dom)

    def via_in(k):
        dst = ext.at[6 - 6 * (k % 2), pl.ds(0, CHUNK)]
        return remote(dst, dst, via_s.at[k % 2], via_r.at[k % 2], partner, row_end[0])

    def via(k, far):
        side = k % 2
        src = ext.at[6 - 6 * side, pl.ds(0, CHUNK)]
        dst = far_in.at[k // 4] if far else ext.at[plane_of(k) + 6 - 8 * side, rows_of(k)]
        return remote(src, dst, via_s.at[side], halo_r.at[k], partner, row_end[side])

    def twin_sum():
        return remote(acc_twin, twin_in, t_s.at[0], t_r.at[0], twin, dom)

    def to_pair(k):
        return remote(own(k), other.at[plane_of(k), rows_of(k), pl.ds(0, 128)], pair_s.at[k], pair_r.at[k], partner, dom)

    def to_cross(k):
        return remote(own(k), other.at[plane_of(k), rows_of(k), pl.ds(128, 128)], cross_s.at[k], cross_r.at[k], cross, dom)

    load(orb_hbm, nat, in_sem, 0).start()
    load(proj_hbm, pnat, pin_sem, 0).start()

    barrier = pltpu.get_barrier_semaphore()
    peers = [(band, x_peer(j)) for j in (1, 2, 3)]
    peers += [(band, yz_peer(j)) for j in range(1, 8)]
    peers += [(partner, dom), (cross, dom)]
    for peer in peers:
        pl.semaphore_signal(barrier, inc=1, device_id=peer, device_id_type=MESH)

    def greet(peer):
        pl.semaphore_signal(barrier, inc=1, device_id=peer, device_id_type=MESH)

    up_end = is_even & (xx == 3)
    down_end = is_even & (xx == 0)
    ahead = lax.rem(yz + 1, 8)
    back = lax.rem(yz + 7, 8)

    for column, chunks in HANDED_ON.items():

        @pl.when(is_odd & (xx == column))
        def _():
            for k, flag in chunks:
                greet((other_odd(flag, 1 - zl), other_yz * 4 + 3 * (k % 2)))
                greet((partner, row_end[k % 2]))

    for end, side, last in ((up_end, 1, ahead), (down_end, 0, back)):

        @pl.when(end)
        def _():
            for b in (band, twin):
                greet((b, lax.rem(dom + 31 + 2 * side, 32)))
            for column, chunks in HANDED_ON.items():
                for k, flag in chunks:
                    if k % 2 == side:
                        greet((other_odd(flag, zl), other_yz * 4 + column))
                    else:
                        greet((partner, (last + 1 - 2 * lax.rem(last, 2)) * 4 + column))

    row = lax.broadcasted_iota(jnp.int32, (256, 256), 0)
    col = lax.broadcasted_iota(jnp.int32, (256, 256), 1)
    gap = (row - col) & 255
    near_z = (gap == 1) | (gap == 255)
    far_z = (gap == 2) | (gap == 254)
    circ[...] = jnp.where(gap == 0, W_CENTER, jnp.where(near_z, W_NEAR, jnp.where(far_z, W_FAR, 0.0))).astype(jnp.bfloat16)
    coef[...] = jnp.zeros_like(coef)
    rc[...] = jnp.zeros_like(rc)

    at_end = up_end | down_end
    def relayout(i):
        load(orb_hbm, nat, in_sem, i).wait()
        slot, k = lax.rem(i, 2), own_order(i)
        px, rows = plane_of(k) + 2, rows_of(k)

        @pl.loop(0, 8)
        def _(q):
            r = pl.ds(pl.multiple_of(q * 16, 16), 16)
            ext[px, rows, r, :] = jnp.swapaxes(nat[slot, r], 0, 1)

    load(orb_hbm, nat, in_sem, 1).start()
    relayout(0)

    edge = (xx == 0) | (xx == 3)
    kinds = (
        (at_end, 8),
        (is_odd & edge, 2),
        (is_odd & jnp.logical_not(edge), 4),
        (is_even & jnp.logical_not(edge), 0),
    )
    for kind, count in kinds:

        @pl.when(kind)
        def _():
            pl.semaphore_wait(barrier, len(peers) + count)

    @pl.loop(0, PARTS)
    def _(i):
        slot = lax.rem(i, 2)
        k = own_order(i)

        @pl.when(i + 1 < PARTS)
        def _():
            load(proj_hbm, pnat, pin_sem, i + 1).start()

        @pl.when((i >= 1) & (i + 1 < PARTS))
        def _():
            load(orb_hbm, nat, in_sem, i + 1).start()

        @pl.when(i >= 1)
        def _():
            relayout(i)

        px = plane_of(k) + 2

        @pl.when(is_even)
        def _():
            for column, chunks in HANDED_ON.items():
                for c, flag in chunks:

                    @pl.when((up_end if c % 2 else down_end) & (k == c))
                    def _():
                        to_via(c, flag, column).start()

            straight = (down_end & (k == 6)) | (up_end & (k == 5))
            across = (down_end & (slot == 0)) | (up_end & (slot == 1))

            @pl.when(straight & (zl == 0))
            def _():
                to_twin(k).start()

            @pl.when(jnp.logical_not(across) | (straight & (zl == 1)))
            def _():
                halo(k).start()

        @pl.when(is_odd)
        def _():
            to_cross(k).start()
            to_pair(k).start()

        load(proj_hbm, pnat, pin_sem, i).wait()

        @pl.loop(0, 8)
        def _(q):
            r = pl.ds(pl.multiple_of(q * 16, 16), 16)
            pt[:, r, :] = jnp.swapaxes(pnat[slot, r], 0, 1)

        first = first_row(k)
        part = coef[...]
        for r in range(CHUNK):
            part = part + dot_rows(pt[r], ext[px, first + r])
        coef[...] = part

    @pl.when(down_end)
    def _():
        ext[0:2, pl.ds(pl.multiple_of(CHUNK * zl, CHUNK), CHUNK), :, :] = jnp.zeros((2, CHUNK, 128, 256), jnp.bfloat16)

    @pl.when(up_end)
    def _():
        ext[6:8, pl.ds(pl.multiple_of(CHUNK * (1 - zl), CHUNK), CHUNK), :, :] = jnp.zeros((2, CHUNK, 128, 256), jnp.bfloat16)

    for d in range(32):
        rc[d % 4, d // 4, 0:4, :] = coef[4 * d:4 * d + 4, :]

    def c1(j):
        return remote(rc.at[lax.rem(xx + j, 4)], s1c.at[j], c1_s.at[j], c1_r.at[j], band, x_peer(j))

    def c2(j):
        return remote(qc.at[lax.rem(yz + j, 8)], s2c.at[j], c2_s.at[j], c2_r.at[j], band, yz_peer(j))

    def n_pair():
        return remote(tc, nb.at[0], n_s.at[0], n_r.at[0], partner, dom)

    def n_cross():
        return remote(tc, nb.at[1], n_s.at[1], n_r.at[1], cross, dom)

    for j in (1, 2, 3):
        c1(j).start()

    def local_rows(start, stop):
        def body(k, carry):
            x = k // 32
            y = lax.rem(k, 32)

            def at(dx, dy):
                return ext[x + 2 + dx, lax.rem(y + 32 + dy, 32)].astype(jnp.float32)

            center = ext[x + 2, y]
            own_z = jnp.dot(center, circ[...], preferred_element_type=jnp.float32)
            near = (at(-1, 0) + at(1, 0)) + (at(0, -1) + at(0, 1))
            far = (at(-2, 0) + at(2, 0)) + (at(0, -2) + at(0, 2))
            kinetic = (own_z + W_NEAR * near + far) * W_SCALE
            img[x, y] = (kinetic + pot[x, pl.ds(y, 1), :] * center.astype(jnp.float32)).astype(jnp.bfloat16)
            return carry

        lax.fori_loop(start, stop, body, 0)

    def first_planes():
        for k in (1, 3, 5, 7):
            halo(k).wait_recv()
        local_rows(0, 64)

    def last_planes():
        for k in (0, 2, 4, 6):
            halo(k).wait_recv()
        local_rows(64, 128)

    @pl.when(down_end)
    def _():
        last_planes()

    @pl.when(is_even & (xx != 0))
    def _():
        first_planes()

    def sum_c1():
        for j in (1, 2, 3):
            c1(j).wait_recv()
        qc[...] = (rc[xx] + s1c[1]) + (s1c[2] + s1c[3])
        for j in range(1, 8):
            c2(j).start()

    def sum_c2():
        for j in range(1, 8):
            c2(j).wait_recv()
        total = qc[yz]
        for j in range(1, 8):
            total = total + s2c[j]
        tc[...] = total

    for column, chunks in HANDED_ON.items():

        for z in range(2):

            @pl.when(is_odd & (xx == column) & (zl == z))
            def _():
                for k, flag in chunks:
                    via_in(k).wait_recv()
                    via(k, flag == (z == 1)).start()

    @pl.when(is_odd)
    def _():
        sum_c1()
        sum_c2()
        n_pair().start()
        n_cross().start()

    def weighted(tile):
        r = lax.broadcasted_iota(jnp.int32, (8, 128), 0)
        scale = jnp.zeros((8, 128), jnp.float32)
        for q in range(4):
            scale = jnp.where(r == q, coupling[4 * dom + q], scale)
        return (scale * tile).astype(jnp.bfloat16).astype(jnp.float32)

    def outer(left, right):
        return lax.dot_general(
            left, right, (((0,), (0,)), ((), ())),
            precision=lax.Precision.HIGHEST, preferred_element_type=jnp.float32,
        )

    def f1(j):
        return remote(rr.at[lax.rem(xx + j, 4)], s1.at[j], f1_s.at[j], f1_r.at[j], band, x_peer(j))

    def f2_own(j):
        return remote(qq.at[0, lax.rem(yz + j, 8)], s2.at[j], f2_s.at[j], f2_r.at[j], band, yz_peer(j))

    def f2_cross(j):
        return remote(qq.at[1, lax.rem(yz + j, 8)], s2.at[j], f2_s.at[8 + j], f2_r.at[j], cross, yz_peer(j))

    @pl.when(down_end)
    def _():
        first_planes()

    @pl.when(is_even & (xx != 0))
    def _():
        last_planes()

    @pl.when(is_even)
    def _():
        sum_c1()
        acc[...] = jnp.zeros_like(acc)

        def products(i):
            k = pair_order(i)
            to_pair(k).wait_recv()
            to_cross(k).wait_recv()
            x = plane_of(k)
            first = first_row(k)

            @pl.loop(0, CHUNK // 4)
            def _(q):
                part = acc[...]
                for r in range(4):
                    y = first + q * 4 + r
                    left = jnp.concatenate([ext[x + 2, y], img[x, y]], axis=0)
                    part = part + dot_rows(left, other[x, y])
                acc[...] = part

        pl.loop(0, 4)(products)

        def twin_products(first, outer_plane, inner_plane, near_at, far_at):
            acc_twin[...] = jnp.zeros_like(acc_twin)

            @pl.loop(0, CHUNK)
            def _(r):
                near = far_in[near_at, r].astype(jnp.float32)
                far = far_in[far_at, r].astype(jnp.float32)
                outer_part = ((W_NEAR * near + W_FAR * far) * W_SCALE).astype(jnp.bfloat16)
                inner_part = ((W_FAR * W_SCALE) * near).astype(jnp.bfloat16)
                acc_twin[...] += dot_rows(outer_part, other[outer_plane, first + r]) + dot_rows(
                    inner_part, other[inner_plane, first + r]
                )

            twin_sum().start()

        @pl.when(down_end)
        def _():
            twin_products(CHUNK * zl, 0, 1, 1, 0)

        @pl.when(up_end)
        def _():
            twin_products(CHUNK * (1 - zl), 3, 2, 0, 1)

        pl.loop(4, PARTS)(products)

        @pl.when(at_end)
        def _():
            twin_sum().wait_recv()
            acc[128:256, 0:128] += twin_in[:, 128:256]
            acc[128:256, 128:256] += twin_in[:, 0:128]

        sum_c2()
        n_pair().wait_recv()
        n_cross().wait_recv()
        mine = tc[...]
        acc[128:256, 0:128] += outer(mine, weighted(nb[0]))
        acc[128:256, 128:256] += outer(weighted(mine), nb[1])
        acc[0:128, 128:256] = acc[0:128, 128:256].T
        acc[128:256, 128:256] = acc[128:256, 128:256].T
        for d in range(32):
            for half in range(2):
                cols = slice(128 * half, 128 * half + 128)
                rr[d % 4, half, d // 4, 0:4, :] = acc[4 * d:4 * d + 4, cols]
                rr[d % 4, half, d // 4, 4:8, :] = acc[128 + 4 * d:128 + 4 * d + 4, cols]
        for j in (1, 2, 3):
            f1(j).start()
        for j in (1, 2, 3):
            f1(j).wait_recv()
        qq[...] = (rr[xx] + s1[1]) + (s1[2] + s1[3])
        for j in range(8):
            f2_cross(j).start()
        for j in range(1, 8):
            f2_own(j).start()
        for j in range(1, 8):
            f2_own(j).wait_recv()
        s2[0] = qq[0, yz]

    @pl.when(is_odd)
    def _():
        for j in range(8):
            f2_cross(j).wait_recv()

    total = s2[0]
    for j in range(1, 8):
        total = total + s2[j]
    lane = lax.broadcasted_iota(jnp.int32, (8, 128), 1)
    block = dom // 16
    mask = jnp.where(lane < 64, pattern[block, 0], pattern[block, 1]).astype(jnp.float32)
    total = total * mask
    corr_out[...] = total[0:4]
    ham_out[...] = total[4:8]

    for j in (1, 2, 3):
        c1(j).wait_send()
    for j in range(1, 8):
        c2(j).wait_send()

    @pl.when(is_even)
    def _():
        for k in range(PARTS):
            halo(k).wait_send()
        for j in (1, 2, 3):
            f1(j).wait_send()
        for j in range(8):
            f2_cross(j).wait_send()
        for j in range(1, 8):
            f2_own(j).wait_send()

    @pl.when(is_odd)
    def _():
        for k in range(PARTS):
            to_pair(k).wait_send()
            to_cross(k).wait_send()
        n_pair().wait_send()
        n_cross().wait_send()

    for column, chunks in HANDED_ON.items():

        @pl.when(is_odd & (xx == column))
        def _():
            for k, _flag in chunks:
                via(k, False).wait_send()

    @pl.when(at_end)
    def _():
        twin_sum().wait_send()


def on_device(orbitals, potential, projectors, coupling, pattern):
    f32, bf16 = jnp.float32, jnp.bfloat16
    dma = lambda n: pltpu.SemaphoreType.DMA((n,))
    hbm = pl.BlockSpec(memory_space=pl.ANY)
    vmem = pl.BlockSpec(memory_space=pltpu.VMEM)
    smem = pl.BlockSpec(memory_space=pltpu.SMEM)
    return tuple(pl.pallas_call(
        kernel,
        out_shape=[jax.ShapeDtypeStruct((4, 128), f32)] * 2,
        in_specs=[hbm, hbm, vmem, smem, smem],
        out_specs=[vmem, vmem],
        scratch_shapes=[
            pltpu.VMEM((2, 128, CHUNK, 256), bf16),
            pltpu.VMEM((2, 128, CHUNK, 256), bf16),
            pltpu.VMEM((CHUNK, 128, 256), bf16),
            pltpu.VMEM((PLANES + 4, 32, 128, 256), bf16),
            pltpu.VMEM((2, CHUNK, 128, 256), bf16),
            pltpu.VMEM((PLANES, 32, 128, 256), bf16),
            pltpu.VMEM((PLANES, 32, 256, 256), bf16),
            pltpu.VMEM((256, 256), bf16),
            pltpu.VMEM((128, 128), f32),
            pltpu.VMEM((256, 256), f32),
            pltpu.VMEM((128, 256), f32),
            pltpu.VMEM((128, 256), f32),
            pltpu.VMEM((4, 8, 8, 128), f32),
            pltpu.VMEM((4, 8, 8, 128), f32),
            pltpu.VMEM((8, 8, 128), f32),
            pltpu.VMEM((8, 8, 128), f32),
            pltpu.VMEM((8, 128), f32),
            pltpu.VMEM((2, 8, 128), f32),
            pltpu.VMEM((4, 2, 8, 8, 128), f32),
            pltpu.VMEM((4, 2, 8, 8, 128), f32),
            pltpu.VMEM((2, 8, 8, 128), f32),
            pltpu.VMEM((8, 8, 128), f32),
            dma(2), dma(2), dma(8), dma(8), dma(8), dma(8), dma(8), dma(8),
            dma(4), dma(4), dma(8), dma(8), dma(2), dma(2), dma(4), dma(4), dma(16), dma(8), dma(2), dma(2), dma(1), dma(1),
        ],
        compiler_params=pltpu.CompilerParams(
            collective_id=0, has_side_effects=True, vmem_limit_bytes=58 * 2**20,
        ),
    )(orbitals, projectors, potential, coupling, pattern))


def solution(mesh):
    return jax.shard_map(
        on_device,
        mesh=mesh,
        in_specs=(
            P("band", "dom", None, None),
            P("dom", None, None),
            P(None, "dom", None, None),
            P(),
            P("band", None),
        ),
        out_specs=(P(("band", "dom"), None), P(("band", "dom"), None)),
        check_vma=False,
    )
```

```python
import functools

import jax
import jax.numpy as jnp
from jax import lax
from jax.experimental import pallas as pl
from jax.experimental.pallas import tpu as pltpu
from jax.sharding import PartitionSpec as P

W_CENTER = 90.0
W_NEAR = -16.0
W_FAR = 1.0
W_SCALE = 1.0 / 24.0

MESH = pl.DeviceIdType.MESH

HANDED_ON = {0: ((4, False),), 1: ((0, False), (1, True)), 2: ((2, True), (3, False)), 3: ((7, False),)}
CHUNK = 16
PLANES = 4
PARTS = 8


def dot_rows(left, right):
    return lax.dot_general(left, right, (((1,), (1,)), ((), ())), preferred_element_type=jnp.float32)


def kernel(
    orb_hbm, proj_hbm, pot, coupling, pattern, out,
    nat, pnat, pt, ext, far_in, img, other, circ, coef, acc, acc_twin, twin_in,
    rc, s1c, qc, s2c, tc, nb, rr, s1, qq, s2,
    in_sem, pin_sem, halo_s, halo_r, pair_s, pair_r, cross_s, cross_r,
    c1_s, c1_r, c2_s, c2_r, n_s, n_r, f1_s, f1_r, f2_s, f2_r, via_r, via_s, t_s, t_r,
):
    band = lax.axis_index("band")
    dom = lax.axis_index("dom")
    core = lax.rem(band, 2)
    zh = band // 2
    yz = dom // 4
    zl = lax.rem(yz, 2)
    xx = lax.rem(dom, 4)
    partner = zh * 2 + (1 - core)
    cross = (1 - zh) * 2 + (1 - core)
    twin = (1 - zh) * 2 + core
    other_yz = yz + 1 - 2 * lax.rem(yz, 2)
    row_end = (lax.rem(other_yz * 4 + 31, 32), lax.rem(other_yz * 4 + 4, 32))
    is_even = core == 0
    is_odd = core == 1

    def x_peer(j):
        return yz * 4 + lax.rem(xx + j, 4)

    def yz_peer(j):
        return lax.rem(yz + j, 8) * 4 + xx

    def remote(src, dst, ssem, rsem, to_band, to_dom):
        return pltpu.make_async_remote_copy(
            src_ref=src, dst_ref=dst, send_sem=ssem, recv_sem=rsem,
            device_id=(to_band, to_dom), device_id_type=MESH,
        )

    def plane_of(k):
        return lax.rem(k, 2) * 2 + k // 4

    def first_row(k):
        return (1 - lax.rem(k // 2, 2)) * CHUNK

    def rows_of(k):
        return pl.ds(pl.multiple_of(first_row(k), CHUNK), CHUNK)

    def pair_order(i):
        i = lax.rem(i + 4 * (1 - zl), PARTS)
        return lax.rem(3 * (i // 2), 4) + 4 * lax.rem(i, 2)

    def own_order(i):
        return i + core * (pair_order(i) - i)

    def load(src, dst, sem, i):
        k, slot = own_order(i), lax.rem(i, 2)
        return pltpu.make_async_copy(src.at[:, plane_of(k), rows_of(k), :], dst.at[slot], sem.at[slot])

    def own(k):
        return ext.at[plane_of(k) + 2, rows_of(k)]

    def halo(k):
        side = lax.rem(k, 2)
        to_dom = lax.rem(dom + 31 + 2 * side, 32)
        return remote(own(k), ext.at[plane_of(k) + 6 - 8 * side, rows_of(k)], halo_s.at[k], halo_r.at[k], band, to_dom)

    def other_odd(flag, z):
        far = int(flag) + z - 2 * int(flag) * z
        return partner + far * (cross - partner)

    def to_via(k, flag, column):
        dst = ext.at[6 - 6 * (k % 2), pl.ds(0, CHUNK)]
        return remote(own(k), dst, halo_s.at[k], via_r.at[k % 2], other_odd(flag, zl), other_yz * 4 + column)

    def to_twin(k):
        to_dom = lax.rem(dom + 31 + 2 * lax.rem(k, 2), 32)
        return remote(own(k), far_in.at[k // 4], halo_s.at[k], halo_r.at[k], twin, to_dom)

    def via_in(k):
        dst = ext.at[6 - 6 * (k % 2), pl.ds(0, CHUNK)]
        return remote(dst, dst, via_s.at[k % 2], via_r.at[k % 2], partner, row_end[0])

    def via(k, far):
        side = k % 2
        src = ext.at[6 - 6 * side, pl.ds(0, CHUNK)]
        dst = far_in.at[k // 4] if far else ext.at[plane_of(k) + 6 - 8 * side, rows_of(k)]
        return remote(src, dst, via_s.at[side], halo_r.at[k], partner, row_end[side])

    def twin_sum():
        return remote(acc_twin, twin_in, t_s.at[0], t_r.at[0], twin, dom)

    def to_pair(k):
        return remote(own(k), other.at[plane_of(k), rows_of(k), pl.ds(0, 128)], pair_s.at[k], pair_r.at[k], partner, dom)

    def to_cross(k):
        return remote(own(k), other.at[plane_of(k), rows_of(k), pl.ds(128, 128)], cross_s.at[k], cross_r.at[k], cross, dom)

    load(orb_hbm, nat, in_sem, 0).start()
    load(proj_hbm, pnat, pin_sem, 0).start()

    barrier = pltpu.get_barrier_semaphore()
    peers = [(band, x_peer(j)) for j in (1, 2, 3)]
    peers += [(band, yz_peer(j)) for j in range(1, 8)]
    peers += [(partner, dom), (cross, dom)]
    for peer in peers:
        pl.semaphore_signal(barrier, inc=1, device_id=peer, device_id_type=MESH)

    def greet(peer):
        pl.semaphore_signal(barrier, inc=1, device_id=peer, device_id_type=MESH)

    up_end = is_even & (xx == 3)
    down_end = is_even & (xx == 0)
    ahead = lax.rem(yz + 1, 8)
    back = lax.rem(yz + 7, 8)

    for column, chunks in HANDED_ON.items():

        @pl.when(is_odd & (xx == column))
        def _():
            for k, flag in chunks:
                greet((other_odd(flag, 1 - zl), other_yz * 4 + 3 * (k % 2)))
                greet((partner, row_end[k % 2]))

    for end, side, last in ((up_end, 1, ahead), (down_end, 0, back)):

        @pl.when(end)
        def _():
            for b in (band, twin):
                greet((b, lax.rem(dom + 31 + 2 * side, 32)))
            for column, chunks in HANDED_ON.items():
                for k, flag in chunks:
                    if k % 2 == side:
                        greet((other_odd(flag, zl), other_yz * 4 + column))
                    else:
                        greet((partner, (last + 1 - 2 * lax.rem(last, 2)) * 4 + column))

    row = lax.broadcasted_iota(jnp.int32, (256, 256), 0)
    col = lax.broadcasted_iota(jnp.int32, (256, 256), 1)
    gap = (row - col) & 255
    near_z = (gap == 1) | (gap == 255)
    far_z = (gap == 2) | (gap == 254)
    circ[...] = jnp.where(gap == 0, W_CENTER, jnp.where(near_z, W_NEAR, jnp.where(far_z, W_FAR, 0.0))).astype(jnp.bfloat16)
    coef[...] = jnp.zeros_like(coef)
    rc[...] = jnp.zeros_like(rc)

    at_end = up_end | down_end
    def relayout(i):
        load(orb_hbm, nat, in_sem, i).wait()
        slot, k = lax.rem(i, 2), own_order(i)
        px, rows = plane_of(k) + 2, rows_of(k)

        @pl.loop(0, 8)
        def _(q):
            r = pl.ds(pl.multiple_of(q * 16, 16), 16)
            ext[px, rows, r, :] = jnp.swapaxes(nat[slot, r], 0, 1)

    load(orb_hbm, nat, in_sem, 1).start()
    relayout(0)

    edge = (xx == 0) | (xx == 3)
    kinds = (
        (at_end, 8),
        (is_odd & edge, 2),
        (is_odd & jnp.logical_not(edge), 4),
        (is_even & jnp.logical_not(edge), 0),
    )
    for kind, count in kinds:

        @pl.when(kind)
        def _():
            pl.semaphore_wait(barrier, len(peers) + count)

    @pl.loop(0, PARTS)
    def _(i):
        slot = lax.rem(i, 2)
        k = own_order(i)

        @pl.when(i + 1 < PARTS)
        def _():
            load(proj_hbm, pnat, pin_sem, i + 1).start()

        @pl.when((i >= 1) & (i + 1 < PARTS))
        def _():
            load(orb_hbm, nat, in_sem, i + 1).start()

        @pl.when(i >= 1)
        def _():
            relayout(i)

        px = plane_of(k) + 2

        @pl.when(is_even)
        def _():
            for column, chunks in HANDED_ON.items():
                for c, flag in chunks:

                    @pl.when((up_end if c % 2 else down_end) & (k == c))
                    def _():
                        to_via(c, flag, column).start()

            straight = (down_end & (k == 6)) | (up_end & (k == 5))
            across = (down_end & (slot == 0)) | (up_end & (slot == 1))

            @pl.when(straight & (zl == 0))
            def _():
                to_twin(k).start()

            @pl.when(jnp.logical_not(across) | (straight & (zl == 1)))
            def _():
                halo(k).start()

        @pl.when(is_odd)
        def _():
            to_cross(k).start()
            to_pair(k).start()

        load(proj_hbm, pnat, pin_sem, i).wait()

        @pl.loop(0, 8)
        def _(q):
            r = pl.ds(pl.multiple_of(q * 16, 16), 16)
            pt[:, r, :] = jnp.swapaxes(pnat[slot, r], 0, 1)

        first = first_row(k)
        part = coef[...]
        for r in range(CHUNK):
            part = part + dot_rows(pt[r], ext[px, first + r])
        coef[...] = part

    @pl.when(down_end)
    def _():
        ext[0:2, pl.ds(pl.multiple_of(CHUNK * zl, CHUNK), CHUNK), :, :] = jnp.zeros((2, CHUNK, 128, 256), jnp.bfloat16)

    @pl.when(up_end)
    def _():
        ext[6:8, pl.ds(pl.multiple_of(CHUNK * (1 - zl), CHUNK), CHUNK), :, :] = jnp.zeros((2, CHUNK, 128, 256), jnp.bfloat16)

    for d in range(32):
        rc[d % 4, d // 4, 0:4, :] = coef[4 * d:4 * d + 4, :]

    def c1(j):
        return remote(rc.at[lax.rem(xx + j, 4)], s1c.at[j], c1_s.at[j], c1_r.at[j], band, x_peer(j))

    def c2(j):
        return remote(qc.at[lax.rem(yz + j, 8)], s2c.at[j], c2_s.at[j], c2_r.at[j], band, yz_peer(j))

    def n_pair():
        return remote(tc, nb.at[0], n_s.at[0], n_r.at[0], partner, dom)

    def n_cross():
        return remote(tc, nb.at[1], n_s.at[1], n_r.at[1], cross, dom)

    for j in (1, 2, 3):
        c1(j).start()

    def local_rows(start, stop):
        def body(k, carry):
            x = k // 32
            y = lax.rem(k, 32)

            def at(dx, dy):
                return ext[x + 2 + dx, lax.rem(y + 32 + dy, 32)].astype(jnp.float32)

            center = ext[x + 2, y]
            own_z = jnp.dot(center, circ[...], preferred_element_type=jnp.float32)
            near = (at(-1, 0) + at(1, 0)) + (at(0, -1) + at(0, 1))
            far = (at(-2, 0) + at(2, 0)) + (at(0, -2) + at(0, 2))
            kinetic = (own_z + W_NEAR * near + far) * W_SCALE
            img[x, y] = (kinetic + pot[x, pl.ds(y, 1), :] * center.astype(jnp.float32)).astype(jnp.bfloat16)
            return carry

        lax.fori_loop(start, stop, body, 0)

    def first_planes():
        for k in (1, 3, 5, 7):
            halo(k).wait_recv()
        local_rows(0, 64)

    def last_planes():
        for k in (0, 2, 4, 6):
            halo(k).wait_recv()
        local_rows(64, 128)

    @pl.when(down_end)
    def _():
        last_planes()

    @pl.when(is_even & (xx != 0))
    def _():
        first_planes()

    def sum_c1():
        for j in (1, 2, 3):
            c1(j).wait_recv()
        qc[...] = (rc[xx] + s1c[1]) + (s1c[2] + s1c[3])
        for j in range(1, 8):
            c2(j).start()

    def sum_c2():
        for j in range(1, 8):
            c2(j).wait_recv()
        total = qc[yz]
        for j in range(1, 8):
            total = total + s2c[j]
        tc[...] = total

    for column, chunks in HANDED_ON.items():

        for z in range(2):

            @pl.when(is_odd & (xx == column) & (zl == z))
            def _():
                for k, flag in chunks:
                    via_in(k).wait_recv()
                    via(k, flag == (z == 1)).start()

    @pl.when(is_odd)
    def _():
        sum_c1()
        sum_c2()
        n_pair().start()
        n_cross().start()

    def weighted(tile):
        r = lax.broadcasted_iota(jnp.int32, (8, 128), 0)
        scale = jnp.zeros((8, 128), jnp.float32)
        for q in range(4):
            scale = jnp.where(r == q, coupling[4 * dom + q], scale)
        return (scale * tile).astype(jnp.bfloat16).astype(jnp.float32)

    def outer(left, right):
        return lax.dot_general(
            left, right, (((0,), (0,)), ((), ())),
            precision=lax.Precision.HIGHEST, preferred_element_type=jnp.float32,
        )

    def f1(j):
        return remote(rr.at[lax.rem(xx + j, 4)], s1.at[j], f1_s.at[j], f1_r.at[j], band, x_peer(j))

    def f2_own(j):
        return remote(qq.at[0, lax.rem(yz + j, 8)], s2.at[j], f2_s.at[j], f2_r.at[j], band, yz_peer(j))

    def f2_cross(j):
        return remote(qq.at[1, lax.rem(yz + j, 8)], s2.at[j], f2_s.at[8 + j], f2_r.at[j], cross, yz_peer(j))

    @pl.when(down_end)
    def _():
        first_planes()

    @pl.when(is_even & (xx != 0))
    def _():
        last_planes()

    @pl.when(is_even)
    def _():
        sum_c1()
        acc[...] = jnp.zeros_like(acc)

        def products(i):
            k = pair_order(i)
            to_pair(k).wait_recv()
            to_cross(k).wait_recv()
            x = plane_of(k)
            first = first_row(k)

            @pl.loop(0, CHUNK // 4)
            def _(q):
                part = acc[...]
                for r in range(4):
                    y = first + q * 4 + r
                    left = jnp.concatenate([ext[x + 2, y], img[x, y]], axis=0)
                    part = part + dot_rows(left, other[x, y])
                acc[...] = part

        pl.loop(0, 4)(products)

        def twin_products(first, outer_plane, inner_plane, near_at, far_at):
            acc_twin[...] = jnp.zeros_like(acc_twin)

            @pl.loop(0, CHUNK)
            def _(r):
                near = far_in[near_at, r].astype(jnp.float32)
                far = far_in[far_at, r].astype(jnp.float32)
                outer_part = ((W_NEAR * near + W_FAR * far) * W_SCALE).astype(jnp.bfloat16)
                inner_part = ((W_FAR * W_SCALE) * near).astype(jnp.bfloat16)
                acc_twin[...] += dot_rows(outer_part, other[outer_plane, first + r]) + dot_rows(
                    inner_part, other[inner_plane, first + r]
                )

            twin_sum().start()

        @pl.when(down_end)
        def _():
            twin_products(CHUNK * zl, 0, 1, 1, 0)

        @pl.when(up_end)
        def _():
            twin_products(CHUNK * (1 - zl), 3, 2, 0, 1)

        pl.loop(4, PARTS)(products)

        @pl.when(at_end)
        def _():
            twin_sum().wait_recv()
            acc[128:256, 0:128] += twin_in[:, 128:256]
            acc[128:256, 128:256] += twin_in[:, 0:128]

        sum_c2()
        n_pair().wait_recv()
        n_cross().wait_recv()
        mine = tc[...]
        acc[128:256, 0:128] += outer(mine, weighted(nb[0]))
        acc[128:256, 128:256] += outer(weighted(mine), nb[1])
        acc[0:128, 128:256] = acc[0:128, 128:256].T
        acc[128:256, 128:256] = acc[128:256, 128:256].T
        for d in range(32):
            for half in range(2):
                cols = slice(128 * half, 128 * half + 128)
                rr[d % 4, half, d // 4, 0:4, :] = acc[4 * d:4 * d + 4, cols]
                rr[d % 4, half, d // 4, 4:8, :] = acc[128 + 4 * d:128 + 4 * d + 4, cols]
        for j in (1, 2, 3):
            f1(j).start()
        for j in (1, 2, 3):
            f1(j).wait_recv()
        qq[...] = (rr[xx] + s1[1]) + (s1[2] + s1[3])
        for j in range(8):
            f2_cross(j).start()
        for j in range(1, 8):
            f2_own(j).start()
        for j in range(1, 8):
            f2_own(j).wait_recv()
        s2[0] = qq[0, yz]

    @pl.when(is_odd)
    def _():
        for j in range(8):
            f2_cross(j).wait_recv()

    total = s2[0]
    for j in range(1, 8):
        total = total + s2[j]
    lane = lax.broadcasted_iota(jnp.int32, (8, 128), 1)
    block = dom // 16
    mask = jnp.where(lane < 64, pattern[block, 0], pattern[block, 1]).astype(jnp.float32)
    total = total * mask
    out[...] = total

    for j in (1, 2, 3):
        c1(j).wait_send()
    for j in range(1, 8):
        c2(j).wait_send()

    @pl.when(is_even)
    def _():
        for k in range(PARTS):
            halo(k).wait_send()
        for j in (1, 2, 3):
            f1(j).wait_send()
        for j in range(8):
            f2_cross(j).wait_send()
        for j in range(1, 8):
            f2_own(j).wait_send()

    @pl.when(is_odd)
    def _():
        for k in range(PARTS):
            to_pair(k).wait_send()
            to_cross(k).wait_send()
        n_pair().wait_send()
        n_cross().wait_send()

    for column, chunks in HANDED_ON.items():

        @pl.when(is_odd & (xx == column))
        def _():
            for k, _flag in chunks:
                via(k, False).wait_send()

    @pl.when(at_end)
    def _():
        twin_sum().wait_send()


def on_device(orbitals, potential, projectors, coupling, pattern):
    f32, bf16 = jnp.float32, jnp.bfloat16
    dma = lambda n: pltpu.SemaphoreType.DMA((n,))
    hbm = pl.BlockSpec(memory_space=pl.ANY)
    vmem = pl.BlockSpec(memory_space=pltpu.VMEM)
    smem = pl.BlockSpec(memory_space=pltpu.SMEM)
    total = pl.pallas_call(
        kernel,
        out_shape=jax.ShapeDtypeStruct((8, 128), f32),
        in_specs=[hbm, hbm, vmem, smem, smem],
        out_specs=vmem,
        scratch_shapes=[
            pltpu.VMEM((2, 128, CHUNK, 256), bf16),
            pltpu.VMEM((2, 128, CHUNK, 256), bf16),
            pltpu.VMEM((CHUNK, 128, 256), bf16),
            pltpu.VMEM((PLANES + 4, 32, 128, 256), bf16),
            pltpu.VMEM((2, CHUNK, 128, 256), bf16),
            pltpu.VMEM((PLANES, 32, 128, 256), bf16),
            pltpu.VMEM((PLANES, 32, 256, 256), bf16),
            pltpu.VMEM((256, 256), bf16),
            pltpu.VMEM((128, 128), f32),
            pltpu.VMEM((256, 256), f32),
            pltpu.VMEM((128, 256), f32),
            pltpu.VMEM((128, 256), f32),
            pltpu.VMEM((4, 8, 8, 128), f32),
            pltpu.VMEM((4, 8, 8, 128), f32),
            pltpu.VMEM((8, 8, 128), f32),
            pltpu.VMEM((8, 8, 128), f32),
            pltpu.VMEM((8, 128), f32),
            pltpu.VMEM((2, 8, 128), f32),
            pltpu.VMEM((4, 2, 8, 8, 128), f32),
            pltpu.VMEM((4, 2, 8, 8, 128), f32),
            pltpu.VMEM((2, 8, 8, 128), f32),
            pltpu.VMEM((8, 8, 128), f32),
            dma(2), dma(2), dma(8), dma(8), dma(8), dma(8), dma(8), dma(8),
            dma(4), dma(4), dma(8), dma(8), dma(2), dma(2), dma(4), dma(4), dma(16), dma(8), dma(2), dma(2), dma(1), dma(1),
        ],
        compiler_params=pltpu.CompilerParams(
            collective_id=0, has_side_effects=True, vmem_limit_bytes=58 * 2**20,
        ),
    )(orbitals, projectors, potential, coupling, pattern)
    return total[0:4], total[4:8]


def solution(mesh):
    return jax.shard_map(
        on_device,
        mesh=mesh,
        in_specs=(
            P("band", "dom", None, None),
            P("dom", None, None),
            P(None, "dom", None, None),
            P(),
            P("band", None),
        ),
        out_specs=(P(("band", "dom"), None), P(("band", "dom"), None)),
        check_vma=False,
    )
```

```python
import functools

import jax
import jax.numpy as jnp
from jax import lax
from jax.experimental import pallas as pl
from jax.experimental.pallas import tpu as pltpu
from jax.sharding import PartitionSpec as P

W_CENTER = 90.0
W_NEAR = -16.0
W_FAR = 1.0
W_SCALE = 1.0 / 24.0

MESH = pl.DeviceIdType.MESH

HANDED_ON = {0: ((4, False),), 1: ((0, False), (1, True)), 2: ((2, True), (3, False)), 3: ((7, False),)}
CHUNK = 16
PLANES = 4
PARTS = 8


def dot_rows(left, right):
    return lax.dot_general(left, right, (((1,), (1,)), ((), ())), preferred_element_type=jnp.float32)


def kernel(
    orb_hbm, proj_hbm, pot_hbm, coupling, pattern, out,
    pot, nat, pnat, pt, ext, far_in, img, other, circ, coef, acc, acc_twin, twin_in,
    rc, s1c, qc, s2c, tc, nb, rr, s1, qq, s2,
    in_sem, pin_sem, halo_s, halo_r, pair_s, pair_r, cross_s, cross_r,
    c1_s, c1_r, c2_s, c2_r, n_s, n_r, f1_s, f1_r, f2_s, f2_r, via_r, via_s, t_s, t_r, pot_sem,
):
    band = lax.axis_index("band")
    dom = lax.axis_index("dom")
    core = lax.rem(band, 2)
    zh = band // 2
    yz = dom // 4
    zl = lax.rem(yz, 2)
    xx = lax.rem(dom, 4)
    partner = zh * 2 + (1 - core)
    cross = (1 - zh) * 2 + (1 - core)
    twin = (1 - zh) * 2 + core
    other_yz = yz + 1 - 2 * lax.rem(yz, 2)
    row_end = (lax.rem(other_yz * 4 + 31, 32), lax.rem(other_yz * 4 + 4, 32))
    is_even = core == 0
    is_odd = core == 1

    def x_peer(j):
        return yz * 4 + lax.rem(xx + j, 4)

    def yz_peer(j):
        return lax.rem(yz + j, 8) * 4 + xx

    def remote(src, dst, ssem, rsem, to_band, to_dom):
        return pltpu.make_async_remote_copy(
            src_ref=src, dst_ref=dst, send_sem=ssem, recv_sem=rsem,
            device_id=(to_band, to_dom), device_id_type=MESH,
        )

    def plane_of(k):
        return lax.rem(k, 2) * 2 + k // 4

    def first_row(k):
        return (1 - lax.rem(k // 2, 2)) * CHUNK

    def rows_of(k):
        return pl.ds(pl.multiple_of(first_row(k), CHUNK), CHUNK)

    def pair_order(i):
        i = lax.rem(i + 4 * (1 - zl), PARTS)
        return lax.rem(3 * (i // 2), 4) + 4 * lax.rem(i, 2)

    def own_order(i):
        return i + core * (pair_order(i) - i)

    def load(src, dst, sem, i):
        k, slot = own_order(i), lax.rem(i, 2)
        return pltpu.make_async_copy(src.at[:, plane_of(k), rows_of(k), :], dst.at[slot], sem.at[slot])

    def own(k):
        return ext.at[plane_of(k) + 2, rows_of(k)]

    def halo(k):
        side = lax.rem(k, 2)
        to_dom = lax.rem(dom + 31 + 2 * side, 32)
        return remote(own(k), ext.at[plane_of(k) + 6 - 8 * side, rows_of(k)], halo_s.at[k], halo_r.at[k], band, to_dom)

    def other_odd(flag, z):
        far = int(flag) + z - 2 * int(flag) * z
        return partner + far * (cross - partner)

    def to_via(k, flag, column):
        dst = ext.at[6 - 6 * (k % 2), pl.ds(0, CHUNK)]
        return remote(own(k), dst, halo_s.at[k], via_r.at[k % 2], other_odd(flag, zl), other_yz * 4 + column)

    def to_twin(k):
        to_dom = lax.rem(dom + 31 + 2 * lax.rem(k, 2), 32)
        return remote(own(k), far_in.at[k // 4], halo_s.at[k], halo_r.at[k], twin, to_dom)

    def via_in(k):
        dst = ext.at[6 - 6 * (k % 2), pl.ds(0, CHUNK)]
        return remote(dst, dst, via_s.at[k % 2], via_r.at[k % 2], partner, row_end[0])

    def via(k, far):
        side = k % 2
        src = ext.at[6 - 6 * side, pl.ds(0, CHUNK)]
        dst = far_in.at[k // 4] if far else ext.at[plane_of(k) + 6 - 8 * side, rows_of(k)]
        return remote(src, dst, via_s.at[side], halo_r.at[k], partner, row_end[side])

    def twin_sum():
        return remote(acc_twin, twin_in, t_s.at[0], t_r.at[0], twin, dom)

    def to_pair(k):
        return remote(own(k), other.at[plane_of(k), rows_of(k), pl.ds(0, 128)], pair_s.at[k], pair_r.at[k], partner, dom)

    def to_cross(k):
        return remote(own(k), other.at[plane_of(k), rows_of(k), pl.ds(128, 128)], cross_s.at[k], cross_r.at[k], cross, dom)

    load(orb_hbm, nat, in_sem, 0).start()
    load(proj_hbm, pnat, pin_sem, 0).start()
    pltpu.make_async_copy(pot_hbm, pot, pot_sem.at[0]).start()

    barrier = pltpu.get_barrier_semaphore()
    peers = [(band, x_peer(j)) for j in (1, 2, 3)]
    peers += [(band, yz_peer(j)) for j in range(1, 8)]
    peers += [(partner, dom), (cross, dom)]
    for peer in peers:
        pl.semaphore_signal(barrier, inc=1, device_id=peer, device_id_type=MESH)

    def greet(peer):
        pl.semaphore_signal(barrier, inc=1, device_id=peer, device_id_type=MESH)

    up_end = is_even & (xx == 3)
    down_end = is_even & (xx == 0)
    ahead = lax.rem(yz + 1, 8)
    back = lax.rem(yz + 7, 8)

    for column, chunks in HANDED_ON.items():

        @pl.when(is_odd & (xx == column))
        def _():
            for k, flag in chunks:
                greet((other_odd(flag, 1 - zl), other_yz * 4 + 3 * (k % 2)))
                greet((partner, row_end[k % 2]))

    for end, side, last in ((up_end, 1, ahead), (down_end, 0, back)):

        @pl.when(end)
        def _():
            for b in (band, twin):
                greet((b, lax.rem(dom + 31 + 2 * side, 32)))
            for column, chunks in HANDED_ON.items():
                for k, flag in chunks:
                    if k % 2 == side:
                        greet((other_odd(flag, zl), other_yz * 4 + column))
                    else:
                        greet((partner, (last + 1 - 2 * lax.rem(last, 2)) * 4 + column))

    row = lax.broadcasted_iota(jnp.int32, (256, 256), 0)
    col = lax.broadcasted_iota(jnp.int32, (256, 256), 1)
    gap = (row - col) & 255
    near_z = (gap == 1) | (gap == 255)
    far_z = (gap == 2) | (gap == 254)
    circ[...] = jnp.where(gap == 0, W_CENTER, jnp.where(near_z, W_NEAR, jnp.where(far_z, W_FAR, 0.0))).astype(jnp.bfloat16)
    coef[...] = jnp.zeros_like(coef)
    rc[...] = jnp.zeros_like(rc)

    at_end = up_end | down_end
    def relayout(i):
        load(orb_hbm, nat, in_sem, i).wait()
        slot, k = lax.rem(i, 2), own_order(i)
        px, rows = plane_of(k) + 2, rows_of(k)

        @pl.loop(0, 8)
        def _(q):
            r = pl.ds(pl.multiple_of(q * 16, 16), 16)
            ext[px, rows, r, :] = jnp.swapaxes(nat[slot, r], 0, 1)

    load(orb_hbm, nat, in_sem, 1).start()
    relayout(0)

    edge = (xx == 0) | (xx == 3)
    kinds = (
        (at_end, 8),
        (is_odd & edge, 2),
        (is_odd & jnp.logical_not(edge), 4),
        (is_even & jnp.logical_not(edge), 0),
    )
    for kind, count in kinds:

        @pl.when(kind)
        def _():
            pl.semaphore_wait(barrier, len(peers) + count)

    @pl.loop(0, PARTS)
    def _(i):
        slot = lax.rem(i, 2)
        k = own_order(i)

        @pl.when(i + 1 < PARTS)
        def _():
            load(proj_hbm, pnat, pin_sem, i + 1).start()

        @pl.when((i >= 1) & (i + 1 < PARTS))
        def _():
            load(orb_hbm, nat, in_sem, i + 1).start()

        @pl.when(i >= 1)
        def _():
            relayout(i)

        px = plane_of(k) + 2

        @pl.when(is_even)
        def _():
            for column, chunks in HANDED_ON.items():
                for c, flag in chunks:

                    @pl.when((up_end if c % 2 else down_end) & (k == c))
                    def _():
                        to_via(c, flag, column).start()

            straight = (down_end & (k == 6)) | (up_end & (k == 5))
            across = (down_end & (slot == 0)) | (up_end & (slot == 1))

            @pl.when(straight & (zl == 0))
            def _():
                to_twin(k).start()

            @pl.when(jnp.logical_not(across) | (straight & (zl == 1)))
            def _():
                halo(k).start()

        @pl.when(is_odd)
        def _():
            to_cross(k).start()
            to_pair(k).start()

        load(proj_hbm, pnat, pin_sem, i).wait()

        @pl.loop(0, 8)
        def _(q):
            r = pl.ds(pl.multiple_of(q * 16, 16), 16)
            pt[:, r, :] = jnp.swapaxes(pnat[slot, r], 0, 1)

        first = first_row(k)
        part = coef[...]
        for r in range(CHUNK):
            part = part + dot_rows(pt[r], ext[px, first + r])
        coef[...] = part

    @pl.when(down_end)
    def _():
        ext[0:2, pl.ds(pl.multiple_of(CHUNK * zl, CHUNK), CHUNK), :, :] = jnp.zeros((2, CHUNK, 128, 256), jnp.bfloat16)

    @pl.when(up_end)
    def _():
        ext[6:8, pl.ds(pl.multiple_of(CHUNK * (1 - zl), CHUNK), CHUNK), :, :] = jnp.zeros((2, CHUNK, 128, 256), jnp.bfloat16)

    pltpu.make_async_copy(pot_hbm, pot, pot_sem.at[0]).wait()

    for d in range(32):
        rc[d % 4, d // 4, 0:4, :] = coef[4 * d:4 * d + 4, :]

    def c1(j):
        return remote(rc.at[lax.rem(xx + j, 4)], s1c.at[j], c1_s.at[j], c1_r.at[j], band, x_peer(j))

    def c2(j):
        return remote(qc.at[lax.rem(yz + j, 8)], s2c.at[j], c2_s.at[j], c2_r.at[j], band, yz_peer(j))

    def n_pair():
        return remote(tc, nb.at[0], n_s.at[0], n_r.at[0], partner, dom)

    def n_cross():
        return remote(tc, nb.at[1], n_s.at[1], n_r.at[1], cross, dom)

    for j in (1, 2, 3):
        c1(j).start()

    def local_rows(start, stop):
        def body(k, carry):
            x = k // 32
            y = lax.rem(k, 32)

            def at(dx, dy):
                return ext[x + 2 + dx, lax.rem(y + 32 + dy, 32)].astype(jnp.float32)

            center = ext[x + 2, y]
            own_z = jnp.dot(center, circ[...], preferred_element_type=jnp.float32)
            near = (at(-1, 0) + at(1, 0)) + (at(0, -1) + at(0, 1))
            far = (at(-2, 0) + at(2, 0)) + (at(0, -2) + at(0, 2))
            kinetic = (own_z + W_NEAR * near + far) * W_SCALE
            img[x, y] = (kinetic + pot[x, pl.ds(y, 1), :] * center.astype(jnp.float32)).astype(jnp.bfloat16)
            return carry

        lax.fori_loop(start, stop, body, 0)

    def first_planes():
        for k in (1, 3, 5, 7):
            halo(k).wait_recv()
        local_rows(0, 64)

    def last_planes():
        for k in (0, 2, 4, 6):
            halo(k).wait_recv()
        local_rows(64, 128)

    @pl.when(down_end)
    def _():
        last_planes()

    @pl.when(is_even & (xx != 0))
    def _():
        first_planes()

    def sum_c1():
        for j in (1, 2, 3):
            c1(j).wait_recv()
        qc[...] = (rc[xx] + s1c[1]) + (s1c[2] + s1c[3])
        for j in range(1, 8):
            c2(j).start()

    def sum_c2():
        for j in range(1, 8):
            c2(j).wait_recv()
        total = qc[yz]
        for j in range(1, 8):
            total = total + s2c[j]
        tc[...] = total

    for column, chunks in HANDED_ON.items():

        for z in range(2):

            @pl.when(is_odd & (xx == column) & (zl == z))
            def _():
                for k, flag in chunks:
                    via_in(k).wait_recv()
                    via(k, flag == (z == 1)).start()

    @pl.when(is_odd)
    def _():
        sum_c1()
        sum_c2()
        n_pair().start()
        n_cross().start()

    def weighted(tile):
        r = lax.broadcasted_iota(jnp.int32, (8, 128), 0)
        scale = jnp.zeros((8, 128), jnp.float32)
        for q in range(4):
            scale = jnp.where(r == q, coupling[4 * dom + q], scale)
        return (scale * tile).astype(jnp.bfloat16).astype(jnp.float32)

    def outer(left, right):
        return lax.dot_general(
            left, right, (((0,), (0,)), ((), ())),
            precision=lax.Precision.HIGHEST, preferred_element_type=jnp.float32,
        )

    def f1(half, j):
        src = rr.at[lax.rem(xx + j, 4), half]
        return remote(src, s1.at[j, half], f1_s.at[4 * half + j], f1_r.at[4 * half + j], band, x_peer(j))

    def f2_own(j):
        return remote(qq.at[0, lax.rem(yz + j, 8)], s2.at[j], f2_s.at[j], f2_r.at[j], band, yz_peer(j))

    def f2_cross(j):
        return remote(qq.at[1, lax.rem(yz + j, 8)], s2.at[j], f2_s.at[8 + j], f2_r.at[j], cross, yz_peer(j))

    @pl.when(down_end)
    def _():
        first_planes()

    @pl.when(is_even & (xx != 0))
    def _():
        last_planes()

    @pl.when(is_even)
    def _():
        sum_c1()
        acc[...] = jnp.zeros_like(acc)

        def products(i):
            k = pair_order(i)
            to_pair(k).wait_recv()
            to_cross(k).wait_recv()
            x = plane_of(k)
            first = first_row(k)

            @pl.loop(0, CHUNK // 4)
            def _(q):
                part = acc[...]
                for r in range(4):
                    y = first + q * 4 + r
                    left = jnp.concatenate([ext[x + 2, y], img[x, y]], axis=0)
                    part = part + dot_rows(left, other[x, y])
                acc[...] = part

        pl.loop(0, 4)(products)

        def twin_products(first, outer_plane, inner_plane, near_at, far_at):
            acc_twin[...] = jnp.zeros_like(acc_twin)

            @pl.loop(0, CHUNK)
            def _(r):
                near = far_in[near_at, r].astype(jnp.float32)
                far = far_in[far_at, r].astype(jnp.float32)
                outer_part = ((W_NEAR * near + W_FAR * far) * W_SCALE).astype(jnp.bfloat16)
                inner_part = ((W_FAR * W_SCALE) * near).astype(jnp.bfloat16)
                acc_twin[...] += dot_rows(outer_part, other[outer_plane, first + r]) + dot_rows(
                    inner_part, other[inner_plane, first + r]
                )

            twin_sum().start()

        @pl.when(down_end)
        def _():
            twin_products(CHUNK * zl, 0, 1, 1, 0)

        @pl.when(up_end)
        def _():
            twin_products(CHUNK * (1 - zl), 3, 2, 0, 1)

        pl.loop(4, PARTS)(products)

        @pl.when(at_end)
        def _():
            twin_sum().wait_recv()
            acc[128:256, 0:128] += twin_in[:, 128:256]
            acc[128:256, 128:256] += twin_in[:, 0:128]

        sum_c2()
        n_pair().wait_recv()
        n_cross().wait_recv()
        mine = tc[...]
        acc[128:256, 0:128] += outer(mine, weighted(nb[0]))
        acc[128:256, 128:256] += outer(weighted(mine), nb[1])
        for half in range(2):
            cols = slice(128 * half, 128 * half + 128)
            if half:
                acc[0:128, cols] = acc[0:128, cols].T
                acc[128:256, cols] = acc[128:256, cols].T
            for d in range(32):
                rr[d % 4, half, d // 4, 0:4, :] = acc[4 * d:4 * d + 4, cols]
                rr[d % 4, half, d // 4, 4:8, :] = acc[128 + 4 * d:128 + 4 * d + 4, cols]
            for j in (2, 1, 3):
                f1(half, j).start()
        for j in (1, 2, 3):
            f1(0, j).wait_recv()
            f1(1, j).wait_recv()
        qq[...] = (rr[xx] + s1[1]) + (s1[2] + s1[3])
        for j in (4, 3, 5, 2, 6, 1, 7, 0):
            f2_cross(j).start()
            if j:
                f2_own(j).start()
        for j in range(1, 8):
            f2_own(j).wait_recv()
        s2[0] = qq[0, yz]

    @pl.when(is_odd)
    def _():
        for j in range(8):
            f2_cross(j).wait_recv()

    total = s2[0]
    for j in range(1, 8):
        total = total + s2[j]
    lane = lax.broadcasted_iota(jnp.int32, (8, 128), 1)
    block = dom // 16
    mask = jnp.where(lane < 64, pattern[block, 0], pattern[block, 1]).astype(jnp.float32)
    total = total * mask
    out[...] = total

    for j in (1, 2, 3):
        c1(j).wait_send()
    for j in range(1, 8):
        c2(j).wait_send()

    @pl.when(is_even)
    def _():
        for k in range(PARTS):
            halo(k).wait_send()
        for j in (1, 2, 3):
            f1(0, j).wait_send()
            f1(1, j).wait_send()
        for j in range(8):
            f2_cross(j).wait_send()
        for j in range(1, 8):
            f2_own(j).wait_send()

    @pl.when(is_odd)
    def _():
        for k in range(PARTS):
            to_pair(k).wait_send()
            to_cross(k).wait_send()
        n_pair().wait_send()
        n_cross().wait_send()

    for column, chunks in HANDED_ON.items():

        @pl.when(is_odd & (xx == column))
        def _():
            for k, _flag in chunks:
                via(k, False).wait_send()

    @pl.when(at_end)
    def _():
        twin_sum().wait_send()


def on_device(orbitals, potential, projectors, coupling, pattern):
    f32, bf16 = jnp.float32, jnp.bfloat16
    dma = lambda n: pltpu.SemaphoreType.DMA((n,))
    hbm = pl.BlockSpec(memory_space=pl.ANY)
    vmem = pl.BlockSpec(memory_space=pltpu.VMEM)
    smem = pl.BlockSpec(memory_space=pltpu.SMEM)
    total = pl.pallas_call(
        kernel,
        out_shape=jax.ShapeDtypeStruct((8, 128), f32),
        in_specs=[hbm, hbm, hbm, smem, smem],
        out_specs=vmem,
        scratch_shapes=[
            pltpu.VMEM((PLANES, 32, 256), f32),
            pltpu.VMEM((2, 128, CHUNK, 256), bf16),
            pltpu.VMEM((2, 128, CHUNK, 256), bf16),
            pltpu.VMEM((CHUNK, 128, 256), bf16),
            pltpu.VMEM((PLANES + 4, 32, 128, 256), bf16),
            pltpu.VMEM((2, CHUNK, 128, 256), bf16),
            pltpu.VMEM((PLANES, 32, 128, 256), bf16),
            pltpu.VMEM((PLANES, 32, 256, 256), bf16),
            pltpu.VMEM((256, 256), bf16),
            pltpu.VMEM((128, 128), f32),
            pltpu.VMEM((256, 256), f32),
            pltpu.VMEM((128, 256), f32),
            pltpu.VMEM((128, 256), f32),
            pltpu.VMEM((4, 8, 8, 128), f32),
            pltpu.VMEM((4, 8, 8, 128), f32),
            pltpu.VMEM((8, 8, 128), f32),
            pltpu.VMEM((8, 8, 128), f32),
            pltpu.VMEM((8, 128), f32),
            pltpu.VMEM((2, 8, 128), f32),
            pltpu.VMEM((4, 2, 8, 8, 128), f32),
            pltpu.VMEM((4, 2, 8, 8, 128), f32),
            pltpu.VMEM((2, 8, 8, 128), f32),
            pltpu.VMEM((8, 8, 128), f32),
            dma(2), dma(2), dma(8), dma(8), dma(8), dma(8), dma(8), dma(8),
            dma(4), dma(4), dma(8), dma(8), dma(2), dma(2), dma(8), dma(8), dma(16), dma(8), dma(2), dma(2), dma(1), dma(1), dma(1),
        ],
        compiler_params=pltpu.CompilerParams(
            collective_id=0, has_side_effects=True, vmem_limit_bytes=58 * 2**20,
        ),
    )(orbitals, projectors, potential, coupling, pattern)
    return total[0:4], total[4:8]


def solution(mesh):
    return jax.shard_map(
        on_device,
        mesh=mesh,
        in_specs=(
            P("band", "dom", None, None),
            P("dom", None, None),
            P(None, "dom", None, None),
            P(),
            P("band", None),
        ),
        out_specs=(P(("band", "dom"), None), P(("band", "dom"), None)),
        check_vma=False,
    )
```
